128 devices in a mesh: gx: 8 (over z_lo, x), gy: 16 (over z_hi, y, core).
Axes of the slice: x: 4, y: 4, z: 4 (z_hi: 2, z_lo: 2; z = z_hi * 2 + z_lo), core: 2. Of those that a mesh axis runs over, the one named last changes fastest.
Arguments:
- flow: float32 [27, 128, 256, 256], P(None, 'gx', 'gy'), may hold values from 0.05 to 0.45
- warmth_populace: float32 [7, 128, 256, 256], P(None, 'gx', 'gy'), as said below
- cell_type: int32 [128, 256, 256], P('gx', 'gy'), may hold values from 0 to 1
Outputs:
- flow_next: float32 [27, 128, 256, 256], P(None, 'gx', 'gy')
- heat_next: float32 [7, 128, 256, 256], P(None, 'gx', 'gy')
- heat_flux: float32 [], replicated
The draws below stay inside these ranges and needn't reach their ends.
Inputs may be any that keep to these rules, and one draw needn't show every extreme that they name: `warmth_populace`: every population is positive.
All inputs are finite; a program needn't handle non-finite values.
Results may differ from the reference program's by a relative error of at most 0.0003.
Values sent between devices are 32-bit elements; how exact they have to be, the bound alone decides.
A program may use at most 128 MiB of HBM per device.

```python
import jax
import jax.numpy as jnp

CZ = 256
STEPS = 2
NX = 128
NY = 256


def geometry(key):
    phase_key = jax.random.fold_in(key, 11)
    rise_key = jax.random.fold_in(key, 13)
    height = jnp.arange(NY, dtype=jnp.int32)[None, :, None]
    along = jnp.arange(CZ, dtype=jnp.int32)[None, None, :]
    wall = max(1, NY // 32)
    pitch = max(4, CZ // 8)
    span = max(1, pitch // 4)
    phase = jax.random.randint(phase_key, (), 0, 2 * pitch)
    place = (along + phase) % (2 * pitch)
    extra = NY // 16 + jax.random.randint(rise_key, (NX, 1, CZ), 0, max(1, NY // 32) + 1)
    low_rib = jnp.where(place < span, extra, 0)
    high_rib = jnp.where((place >= pitch) & (place < pitch + span), extra, 0)
    low = height < wall + low_rib
    high = height >= NY - wall - high_rib
    return (low | high).astype(jnp.int32)


def draw_cell_type(key, part):
    metal = geometry(key)
    return metal


def draw_warmth_populace(key, part):
    metal = geometry(key)
    key = jax.random.fold_in(key, 5)
    weights = jnp.array([0.25, 0.125, 0.125, 0.125, 0.125, 0.125, 0.125], jnp.float32)[:, None, None, None]
    base = jnp.where(metal == 1, 1.5, 0.5).astype(jnp.float32)
    noise = jax.random.uniform(key, (7, NX, NY, CZ), jnp.float32, -0.6, 0.6)
    return (weights * base[None] * (1.0 + noise)).astype(jnp.float32)


def block_scale(key, shape, shards, smallest, largest):
    gain = 1.0
    for dim, parts in shards:
        heights = jax.random.uniform(jax.random.fold_in(jax.random.fold_in(key, 6), dim), (parts,), jnp.float32, smallest / len(shards), largest / len(shards))
        gain = gain * jnp.repeat(jnp.exp(heights), shape[dim] // parts).reshape((-1,) + (1,) * (len(shape) - 1 - dim))
    return gain


def setup_inputs(seed: int = 0) -> dict:
    streams_of = jax.random.split(jax.random.key(seed), 4)
    return {
        "flow": jnp.clip(0.05 + 0.39999999 * jax.random.uniform(streams_of[0], (27, NX, NY, CZ), jnp.float32) ** block_scale(streams_of[0], (27, NX, NY, CZ), ((1, 8), (2, 16)), -0.2, 0.2), 0.05, 0.45),
        "warmth_populace": draw_warmth_populace(jax.random.fold_in(streams_of[3], 71), 0),
        "cell_type": draw_cell_type(jax.random.fold_in(streams_of[3], 71), 0),
    }


FLOW_MOVES = [(a, b, e) for a in (-1, 0, 1) for b in (-1, 0, 1) for e in (-1, 0, 1)]
FLOW_WEIGHTS = [[8.0 / 27.0, 2.0 / 27.0, 1.0 / 54.0, 1.0 / 216.0][abs(a) + abs(b) + abs(e)] for (a, b, e) in FLOW_MOVES]
HEAT_MOVES = [(0, 0, 0), (1, 0, 0), (-1, 0, 0), (0, 1, 0), (0, -1, 0), (0, 0, 1), (0, 0, -1)]
WARMTH_FACTORS = [0.25, 0.125, 0.125, 0.125, 0.125, 0.125, 0.125]
HEAT_OPPOSITE = [0, 2, 1, 4, 3, 6, 5]
kinematic_shear_drag = 0.05
coolant_diffusion = 0.05
metal_diffusion = 0.25


def vertical_strip(values):
    return jnp.array(values, jnp.float32)[:, None, None, None]


def relax(flow, warmth_populace, cell_type):
    fluid = cell_type == 0
    density = jnp.sum(flow, axis=0)
    speeds = []
    for axis_number in range(3):
        table = vertical_strip([float(offset[axis_number]) for offset in FLOW_MOVES])
        moment = jnp.sum(flow * table, axis=0)
        speeds.append(jnp.where(fluid, moment / density, 0.0))
    cellwise_warmth_level = jnp.sum(warmth_populace, axis=0)
    momentum_collision_rate = 0.5 + 3.0 * kinematic_shear_drag * jnp.exp(-0.5 * (cellwise_warmth_level - 1.0))
    squared = speeds[0] * speeds[0] + speeds[1] * speeds[1] + speeds[2] * speeds[2]
    along = (vertical_strip([float(o[0]) for o in FLOW_MOVES]) * speeds[0][None]
             + vertical_strip([float(o[1]) for o in FLOW_MOVES]) * speeds[1][None]
             + vertical_strip([float(o[2]) for o in FLOW_MOVES]) * speeds[2][None])
    balance = vertical_strip(FLOW_WEIGHTS) * density[None] * (1.0 + 3.0 * along + 4.5 * along * along - 1.5 * squared[None])
    collided = jnp.where(fluid[None], flow - (flow - balance) / momentum_collision_rate[None], flow)
    advected_warmth = (vertical_strip([float(o[0]) for o in HEAT_MOVES]) * speeds[0][None]
                  + vertical_strip([float(o[1]) for o in HEAT_MOVES]) * speeds[1][None]
                  + vertical_strip([float(o[2]) for o in HEAT_MOVES]) * speeds[2][None])
    warmth_conservation_check = vertical_strip(WARMTH_FACTORS) * cellwise_warmth_level[None] * (1.0 + 4.0 * advected_warmth)
    tau_heat = jnp.where(fluid, 0.5 + 4.0 * coolant_diffusion, 0.5 + 4.0 * metal_diffusion)
    hot = warmth_populace - (warmth_populace - warmth_conservation_check) / tau_heat[None]
    return collided, hot


def shifted(field, offset, fill):
    rolled = jnp.roll(field, offset[0], axis=0)
    if offset[1] == 1:
        rolled = jnp.concatenate([jnp.full_like(rolled[:, :1], fill), rolled[:, :-1]], axis=1)
    elif offset[1] == -1:
        rolled = jnp.concatenate([rolled[:, 1:], jnp.full_like(rolled[:, :1], fill)], axis=1)
    return jnp.roll(rolled, offset[2], axis=2)


def advance(flow, warmth_populace, cell_type):
    fluid = cell_type == 0
    coded = cell_type + 1
    collided, hot = relax(flow, warmth_populace, cell_type)
    members = []
    for number, offset in enumerate(FLOW_MOVES):
        source = shifted(collided[number], offset, 0.0)
        kinds = shifted(coded, offset, 0)
        members.append(jnp.where(kinds == 1, source, collided[26 - number]))
    flow_next = jnp.where(fluid[None], jnp.stack(members), flow)
    heat_members = []
    flux = jnp.float32(0.0)
    for number, offset in enumerate(HEAT_MOVES):
        source = shifted(hot[number], offset, 0.0)
        kinds = shifted(coded, offset, 0)
        back = hot[HEAT_OPPOSITE[number]]
        heat_members.append(jnp.where(kinds > 0, source, back))
        flux = flux + jnp.sum(jnp.where(fluid & (kinds == 2), source - back, 0.0))
    return flow_next, jnp.stack(heat_members), flux


def reference(flow, warmth_populace, cell_type):
    total = jnp.float32(0.0)
    for turn in range(STEPS):
        flow, warmth_populace, flux = advance(flow, warmth_populace, cell_type)
        total = total + flux
    return flow, warmth_populace, total / float(NX * NY)
```

```python
import functools

import jax
import jax.numpy as jnp
from jax import lax
from jax.experimental import pallas as pl
from jax.experimental.pallas import tpu as pltpu
from jax.sharding import PartitionSpec as P

MESH = pl.DeviceIdType.MESH
STEPS = 2
LANES = 128
ROWS = 8

PAIRS = [
    (a, b, e)
    for a in (-1, 0, 1)
    for b in (-1, 0, 1)
    for e in (-1, 0, 1)
    if (a, b, e) > (0, 0, 0)
]
HEAT_MOVES = [(0, 0, 0), (1, 0, 0), (-1, 0, 0), (0, 1, 0), (0, -1, 0), (0, 0, 1), (0, 0, -1)]
TAU_COOLANT = 0.5 + 4.0 * 0.05
TAU_METAL = 0.5 + 4.0 * 0.25
FACES = [(1, 0), (-1, 0)]
SIDES = [(0, 1), (0, -1)]
CORNERS = [(1, 1), (1, -1), (-1, 1), (-1, -1)]


def first_plane(a):
    return 1 if a == 1 else 0


def first_row(b):
    return ROWS if b == 1 else 0


def tree(terms):
    terms = list(terms)
    while len(terms) > 1:
        terms = [
            terms[k] + terms[k + 1] if k + 1 < len(terms) else terms[k]
            for k in range(0, len(terms), 2)
        ]
    return terms[0]


def signed(terms):
    plus = tree([value for sign, value in terms if sign > 0])
    minus = [value for sign, value in terms if sign < 0]
    return plus - tree(minus) if minus else plus


def inverse(value):
    guess = pl.reciprocal(value, approx=True)
    return guess * (2.0 - value * guess)


def lane_shift(pair, e, lane):
    if e == 0:
        return pair
    turned = [pltpu.roll(half, 1 if e == 1 else LANES - 1, 1) for half in pair]
    at_end = lane == (0 if e == 1 else LANES - 1)
    return [jnp.where(at_end, turned[1 - k], turned[k]) for k in range(2)]


def collide(rest, sums, diffs, heat, fluid):
    density = tree([rest] + sums)
    moments = [
        signed([(c[axis], diffs[k]) for k, c in enumerate(PAIRS) if c[axis] != 0])
        for axis in range(3)
    ]
    warmth = tree(heat)
    rate = inverse(0.5 + 0.15 * jnp.exp(0.5 - 0.5 * warmth))
    rate = jnp.where(fluid, rate, 0.0)
    scale = jnp.where(fluid, inverse(density) * 3.0, 0.0)
    vx, vy, vz = [moment * scale for moment in moments]
    keep = 0.5 - 0.5 * rate
    turn = jnp.where(fluid, keep, -0.5)
    weight = rate * density
    sx, sy, sz = (0.5 * vx) * vx, (0.5 * vy) * vy, (0.5 * vz) * vz
    total = sx + sy + sz
    base = 1.0 - total * (1.0 / 3.0)
    k1 = weight * (2.0 / 27.0)
    k2 = weight * (1.0 / 54.0)
    k3 = weight * (1.0 / 216.0)
    halves = {}
    speed = (vx, vy, vz)
    square = (sx, sy, sz)
    for axis in range(3):
        c = tuple(1 if n == axis else 0 for n in range(3))
        halves[c] = (k1 * (base + square[axis]), k1 * speed[axis])
    k2v = [k2 * v for v in speed]
    for m, n in ((0, 1), (0, 2), (1, 2)):
        even = k2 * (base + square[m] + square[n])
        cross = k2v[m] * speed[n]
        for sign in (1, -1):
            c = [0, 0, 0]
            c[m], c[n] = 1, sign
            halves[tuple(c)] = (
                (even + cross, k2v[m] + k2v[n]) if sign == 1 else (even - cross, k2v[m] - k2v[n])
            )
    k3v = [k3 * v for v in speed]
    even = k3 * (base + total)
    xy, xz, yz = k3v[0] * vy, k3v[0] * vz, k3v[1] * vz
    for b in (1, -1):
        outer = even + xy if b == 1 else even - xy
        inner = xz + yz if b == 1 else xz - yz
        slope = k3v[0] + k3v[1] if b == 1 else k3v[0] - k3v[1]
        for e in (1, -1):
            halves[(1, b, e)] = (
                (outer + inner, slope + k3v[2]) if e == 1 else (outer - inner, slope - k3v[2])
            )
    out_rest = (keep + keep) * rest + (weight * (8.0 / 27.0)) * base
    out_pairs = []
    for k, c in enumerate(PAIRS):
        even, odd = halves[c]
        even = keep * sums[k] + even
        odd = turn * diffs[k] + odd
        out_pairs.append((even + odd, even - odd))
    heat_rate = jnp.where(fluid, 1.0 / TAU_COOLANT, 1.0 / TAU_METAL)
    heat_keep = 1.0 - heat_rate
    part = (heat_rate * 0.125) * warmth
    slant = part * (4.0 / 3.0)
    hot = [heat_keep * heat[0] + (part + part)]
    for axis in range(3):
        lean = slant * speed[axis]
        hot.append(heat_keep * heat[1 + 2 * axis] + (part + lean))
        hot.append(heat_keep * heat[2 + 2 * axis] + (part - lean))
    return out_rest, out_pairs, hot


def step_kernel(
    nx, ny, flow_hbm, heat_hbm, kind_hbm, flow_out, heat_out, flux_out,
    flow_in, heat_in, kind, lines, bits, weights, cold_a, cold_b, warm_a, warm_b, meet, meet2, flux_ref,
    in_sem, kind_sem, send_sem, recv_sem, ksend_sem, krecv_sem, sum_sem, sum_recv,
):
    gx, gy = lax.axis_index("gx"), lax.axis_index("gy")
    planes = flow_in.shape[1]
    height = flow_in.shape[2]
    lane = lax.broadcasted_iota(jnp.int32, (ROWS, LANES), 1)
    half = height // ROWS

    def plane_of(p):
        return lax.rem(p, 2) * (planes - 1 - p // 2) + (1 - lax.rem(p, 2)) * (p // 2)

    def device(dx, dy):
        return (lax.rem(gx + dx + nx, nx), lax.rem(gy + dy + ny, ny))

    def inside(dy, act):
        if dy == 1:
            pl.when(gy < ny - 1)(act)
        elif dy == -1:
            pl.when(gy > 0)(act)
        else:
            act()

    kind_copies = [
        pltpu.make_async_copy(
            kind_hbm.at[:, :, pl.ds(z * LANES, LANES)],
            kind.at[pl.ds(1, planes), z, pl.ds(ROWS, height), :],
            kind_sem.at[z],
        )
        for z in range(2)
    ]
    for copy in kind_copies:
        copy.start()

    def load(p):
        x = plane_of(p)
        return [
            pltpu.make_async_copy(
                flow_hbm.at[:, pl.ds(x, 1)], flow_in.at[:, pl.ds(x, 1)], in_sem.at[0, p]
            ),
            pltpu.make_async_copy(
                heat_hbm.at[:, pl.ds(x, 1)], heat_in.at[:, pl.ds(x, 1)], in_sem.at[1, p]
            ),
        ]

    def load_all(p, carry):
        for copy in load(p):
            copy.start()
        return carry

    lax.fori_loop(0, planes, load_all, 0)

    barrier = pltpu.get_barrier_semaphore()
    for dx, dy in CORNERS:
        pl.semaphore_signal(barrier, inc=1, device_id=device(dx, dy), device_id_type=MESH)
    for d in range(1, nx):
        pl.semaphore_signal(barrier, inc=1, device_id=device(d, 0), device_id_type=MESH)
    for d in range(1, ny):
        pl.semaphore_signal(barrier, inc=1, device_id=device(0, d), device_id_type=MESH)

    for copy in kind_copies:
        copy.wait()

    def kind_copy(n, dx, dy):
        src_x = {1: pl.ds(planes, 1), -1: pl.ds(1, 1), 0: pl.ds(1, planes)}[dx]
        dst_x = {1: pl.ds(0, 1), -1: pl.ds(planes + 1, 1), 0: pl.ds(1, planes)}[dx]
        src_y = {1: pl.ds(ROWS + height - 1, 1), -1: pl.ds(ROWS, 1), 0: pl.ds(ROWS, height)}[dy]
        dst_y = {1: pl.ds(ROWS - 1, 1), -1: pl.ds(ROWS + height, 1), 0: pl.ds(ROWS, height)}[dy]
        return pltpu.make_async_remote_copy(
            src_ref=kind.at[src_x, :, src_y, :],
            dst_ref=kind.at[dst_x, :, dst_y, :],
            send_sem=ksend_sem.at[n],
            recv_sem=krecv_sem.at[n],
            device_id=device(dx, dy),
            device_id_type=MESH,
        )

    kind_list = [(n, dx, dy) for n, (dx, dy) in enumerate(FACES + SIDES + CORNERS)]

    def face_copies(turn, cold, warm, dx):
        n = 0 if dx == 1 else 1
        a = dx + 1
        src = planes if dx == 1 else 0
        dst = 0 if dx == 1 else planes
        j = 1 if dx == 1 else 2
        return [
            pltpu.make_async_remote_copy(
                src_ref=cold.at[a, b, :, src, :, pl.ds(first_row(b - 1), height), :],
                dst_ref=cold.at[a, b, :, dst, :, pl.ds(first_row(b - 1), height), :],
                send_sem=send_sem.at[turn, 4 * n + b],
                recv_sem=recv_sem.at[turn, 4 * n + b],
                device_id=device(dx, 0),
                device_id_type=MESH,
            )
            for b in range(3)
        ] + [
            pltpu.make_async_remote_copy(
                src_ref=warm.at[j, src, :, pl.ds(0, height), :],
                dst_ref=warm.at[j, dst, :, pl.ds(0, height), :],
                send_sem=send_sem.at[turn, 4 * n + 3],
                recv_sem=recv_sem.at[turn, 4 * n + 3],
                device_id=device(dx, 0),
                device_id_type=MESH,
            )
        ]

    def corner_copy(turn, cold, dx, dy):
        n = 8 + CORNERS.index((dx, dy))
        src = planes if dx == 1 else 0
        dst = 0 if dx == 1 else planes
        src_y = ROWS + height - 1 if dy == 1 else 0
        dst_y = ROWS - 1 if dy == 1 else height
        return pltpu.make_async_remote_copy(
            src_ref=cold.at[dx + 1, dy + 1, :, src, :, pl.ds(src_y, 1), :],
            dst_ref=cold.at[dx + 1, dy + 1, :, dst, :, pl.ds(dst_y, 1), :],
            send_sem=send_sem.at[turn, n],
            recv_sem=recv_sem.at[turn, n],
            device_id=device(dx, dy),
            device_id_type=MESH,
        )

    group = 2

    def side_copies(turn, cold, warm, dy, g):
        src_y = ROWS + height - 1 if dy == 1 else 0
        dst_y = ROWS - 1 if dy == 1 else height
        j = 3 if dy == 1 else 4
        at = 12 + 4 * (planes // group) * (0 if dy == 1 else 1) + 4 * g
        copies = []
        for a in range(3):
            xs = pl.ds(first_plane(a - 1) + group * g, group)
            copies.append(
                pltpu.make_async_remote_copy(
                    src_ref=cold.at[a, dy + 1, :, xs, :, pl.ds(src_y, 1), :],
                    dst_ref=cold.at[a, dy + 1, :, xs, :, pl.ds(dst_y, 1), :],
                    send_sem=send_sem.at[turn, at + a],
                    recv_sem=recv_sem.at[turn, at + a],
                    device_id=device(0, dy),
                    device_id_type=MESH,
                )
            )
        xs = pl.ds(group * g, group)
        copies.append(
            pltpu.make_async_remote_copy(
                src_ref=warm.at[j, xs, :, pl.ds(src_y, 1), :],
                dst_ref=warm.at[j, xs, :, pl.ds(dst_y, 1), :],
                send_sem=send_sem.at[turn, at + 3],
                recv_sem=recv_sem.at[turn, at + 3],
                device_id=device(0, dy),
                device_id_type=MESH,
            )
        )
        return copies

    def start_all(copies):
        def act():
            for copy in copies:
                copy.start()
        return act

    def wait_recv_all(copies):
        def act():
            for copy in copies:
                copy.wait_recv()
        return act

    def wait_send_all(copies):
        def act():
            for copy in copies:
                copy.wait_send()
        return act

    def send_faces(turn, cold, warm):
        for dx, _ in FACES:
            start_all(face_copies(turn, cold, warm, dx))()
        for dx, dy in CORNERS:
            inside(dy, start_all([corner_copy(turn, cold, dx, dy)]))

    def take_faces(turn, cold, warm):
        for dx, _ in FACES:
            wait_recv_all(face_copies(turn, cold, warm, dx))()
        for dx, dy in CORNERS:
            inside(-dy, wait_recv_all([corner_copy(turn, cold, dx, dy)]))

    def send_sides(turn, cold, warm, g):
        for _, dy in SIDES:
            inside(dy, start_all(side_copies(turn, cold, warm, dy, g)))

    def take_sides(turn, cold, warm, g):
        for _, dy in SIDES:
            inside(-dy, wait_recv_all(side_copies(turn, cold, warm, dy, g)))

    groups = planes // group

    def sends_after(p, turn, cold, warm):
        @pl.when(p == 1)
        def _():
            send_faces(turn, cold, warm)

        @pl.when(lax.rem(p, 2 * group) == 2 * group - 1)
        def _():
            g = p // (2 * group)
            send_sides(turn, cold, warm, g)
            send_sides(turn, cold, warm, groups - 1 - g)

    def takes_before(p, turn, cold, warm):
        @pl.when(p == 0)
        def _():
            take_faces(turn, cold, warm)
            take_sides(turn, cold, warm, 0)
            take_sides(turn, cold, warm, groups - 1)

        @pl.when((lax.rem(p, 2 * group) == 2 * group - 2) & (p < planes - group))
        def _():
            g = p // (2 * group) + 1
            take_sides(turn, cold, warm, g)
            take_sides(turn, cold, warm, groups - 1 - g)

    def store(cold, warm, x, r, z, rest, pairs, hot):
        cold[1, 1, 1, x, z, pl.ds(r, ROWS), :] = rest
        for (a, b, e), (ahead, back) in zip(PAIRS, pairs):
            for (ca, cb, ce), value in (((a, b, e), ahead), ((-a, -b, -e), back)):
                cold[ca + 1, cb + 1, ce + 1, x + first_plane(ca), z, pl.ds(r + first_row(cb), ROWS), :] = value
        for j, (a, b, e) in enumerate(HEAT_MOVES):
            warm[j, x + first_plane(a), z, pl.ds(r + first_row(b), ROWS), :] = hot[j]

    def wall_rows(warm, x):
        @pl.when(gy == 0)
        def _():
            for z in range(2):
                warm[3, x, z, pl.ds(ROWS - 1, 1), :] = warm[4, x, z, pl.ds(0, 1), :]

        @pl.when(gy == ny - 1)
        def _():
            for z in range(2):
                warm[4, x, z, pl.ds(height, 1), :] = warm[3, x, z, pl.ds(ROWS + height - 1, 1), :]

    def first(p, carry):
        x = plane_of(p)
        for copy in load(p):
            copy.wait()

        @pl.when(p == 1)
        def _():
            pl.semaphore_wait(barrier, len(CORNERS) + nx - 1 + ny - 1)
            for n, dx, dy in kind_list:
                inside(dy, kind_copy(n, dx, dy).start)

        def unit(h, carry):
            r = pl.multiple_of(h * ROWS, ROWS)
            for z in range(2):
                at = (x, pl.ds(r, ROWS), pl.ds(z * LANES, LANES))
                values = [flow_in[(i,) + at] for i in range(27)]
                heat = [heat_in[(j,) + at] for j in range(7)]
                fluid = kind[x + 1, z, pl.ds(r + ROWS, ROWS), :] == 0
                sums = [values[i] + values[26 - i] for i in range(14, 27)]
                diffs = [values[i] - values[26 - i] for i in range(14, 27)]
                rest, pairs, hot = collide(values[13], sums, diffs, heat, fluid)
                store(cold_a, warm_a, x, r, z, rest, pairs, hot)
            return carry

        lax.fori_loop(0, half, unit, 0)
        wall_rows(warm_a, x)
        sends_after(p, 0, cold_a, warm_a)
        return carry

    lax.fori_loop(0, planes, first, 0)

    for n, dx, dy in kind_list:
        inside(-dy, kind_copy(n, dx, dy).wait_recv)

    def outside_rows(row):
        def act():
            kind[:, :, pl.ds(row, 1), :] = jnp.full((planes + 2, 2, 1, LANES), 2, jnp.int32)
        return act

    pl.when(gy == 0)(outside_rows(ROWS - 1))
    pl.when(gy == ny - 1)(outside_rows(ROWS + height))

    def line(u, carry):
        x, r = u // (half + 2), pl.multiple_of(lax.rem(u, half + 2) * ROWS, ROWS)
        here = [(kind[x, z, pl.ds(r, ROWS), :] == 0).astype(jnp.int32) for z in range(2)]
        above = lane_shift(here, -1, lane)
        below = lane_shift(here, 1, lane)
        for z in range(2):
            lines[x, z, pl.ds(r, ROWS), :] = above[z] + 2 * here[z] + 4 * below[z]
        return carry

    lax.fori_loop(0, (planes + 2) * (half + 2), line, 0)

    def mask(u, carry):
        x, r = u // half, pl.multiple_of(lax.rem(u, half) * ROWS, ROWS)
        own = [kind[x + 1, z, pl.ds(r + ROWS, ROWS), :] for z in range(2)]
        around = [
            [kind[x + 2, z, pl.ds(r + ROWS, ROWS), :] for z in range(2)],
            [kind[x, z, pl.ds(r + ROWS, ROWS), :] for z in range(2)],
            [kind[x + 1, z, pl.ds(r + ROWS + 1, ROWS), :] for z in range(2)],
            [kind[x + 1, z, pl.ds(r + ROWS - 1, ROWS), :] for z in range(2)],
            lane_shift(own, -1, lane),
            lane_shift(own, 1, lane),
        ]
        for z in range(2):
            found = jnp.zeros((ROWS, LANES), jnp.int32)
            for a in (-1, 0, 1):
                for b in (-1, 0, 1):
                    found = found + (
                        lines[x + 1 - a, z, pl.ds(r + ROWS - b, ROWS), :] << (9 * (a + 1) + 3 * (b + 1))
                    )
            bits[x, z, pl.ds(r, ROWS), :] = jnp.where(own[z] == 0, found, 0)
            for j in range(6):
                other = jnp.where(around[j][z] == 2, own[z], around[j][z])
                weights[j, x, z, pl.ds(r, ROWS), :] = (own[z] - other).astype(jnp.float32)
        return carry

    lax.fori_loop(0, planes * half, mask, 0)

    def arrive(cold, x, r, code, c):
        a, b, e = c
        number = 9 * (a + 1) + 3 * (b + 1) + (e + 1)
        found = [
            cold[a + 1, b + 1, e + 1, x + first_plane(a) - a, z, pl.ds(r + first_row(b) - b, ROWS), :]
            for z in range(2)
        ]
        found = lane_shift(found, e, lane)
        return [
            jnp.where(
                (code[z] & (1 << number)) != 0,
                found[z],
                cold[1 - a, 1 - b, 1 - e, x + first_plane(-a), z, pl.ds(r + first_row(-b), ROWS), :],
            )
            for z in range(2)
        ]

    def arrive_heat(warm, x, r, j):
        a, b, e = HEAT_MOVES[j]
        found = [
            warm[j, x + first_plane(a) - a, z, pl.ds(r + first_row(b) - b, ROWS), :] for z in range(2)
        ]
        return lane_shift(found, e, lane)

    flux_ref[...] = jnp.zeros_like(flux_ref)

    def second(p, carry):
        x = plane_of(p)
        takes_before(p, 0, cold_a, warm_a)

        def unit(h, carry):
            r = pl.multiple_of(h * ROWS, ROWS)
            code = [bits[x, z, pl.ds(r, ROWS), :] for z in range(2)]
            rest = [cold_a[1, 1, 1, x, z, pl.ds(r, ROWS), :] for z in range(2)]
            sums, diffs = [], []
            for a, b, e in PAIRS:
                ahead = arrive(cold_a, x, r, code, (a, b, e))
                back = arrive(cold_a, x, r, code, (-a, -b, -e))
                sums.append([ahead[z] + back[z] for z in range(2)])
                diffs.append([ahead[z] - back[z] for z in range(2)])
            heat = [arrive_heat(warm_a, x, r, j) for j in range(7)]
            flux = flux_ref[...]
            for z in range(2):
                fluid = kind[x + 1, z, pl.ds(r + ROWS, ROWS), :] == 0
                out_rest, pairs, hot = collide(
                    rest[z], [s[z] for s in sums], [d[z] for d in diffs], [g[z] for g in heat], fluid
                )
                store(cold_b, warm_b, x, r, z, out_rest, pairs, hot)
                terms = []
                for j in range(1, 7):
                    a, b, e = HEAT_MOVES[j]
                    was = warm_a[j, x + first_plane(a), z, pl.ds(r + first_row(b), ROWS), :]
                    terms.append(weights[j - 1, x, z, pl.ds(r, ROWS), :] * (was + hot[j]))
                flux = flux + tree(terms)
            flux_ref[...] = flux
            return carry

        lax.fori_loop(0, half, unit, 0)
        wall_rows(warm_b, x)
        sends_after(p, 1, cold_b, warm_b)
        return carry

    lax.fori_loop(0, planes, second, 0)

    def sum_copies(slots, stage, axis, index, count):
        return [
            pltpu.make_async_remote_copy(
                src_ref=slots.at[index],
                dst_ref=slots.at[index],
                send_sem=sum_sem.at[stage, d - 1],
                recv_sem=sum_recv.at[stage, d - 1],
                device_id=device(d, 0) if axis == 0 else device(0, d),
                device_id_type=MESH,
            )
            for d in range(1, count)
        ]

    meet[gy] = flux_ref[...]
    column = sum_copies(meet, 0, 1, gy, ny)
    start_all(column)()

    def third(p, carry):
        x = plane_of(p)
        takes_before(p, 1, cold_b, warm_b)

        def unit(h, carry):
            r = pl.multiple_of(h * ROWS, ROWS)
            code = [bits[x, z, pl.ds(r, ROWS), :] for z in range(2)]
            for a in (-1, 0, 1):
                for b in (-1, 0, 1):
                    for e in (-1, 0, 1):
                        i = 9 * (a + 1) + 3 * (b + 1) + (e + 1)
                        if i == 13:
                            value = [cold_b[1, 1, 1, x, z, pl.ds(r, ROWS), :] for z in range(2)]
                        else:
                            value = arrive(cold_b, x, r, code, (a, b, e))
                        for z in range(2):
                            flow_out[i, x, pl.ds(r, ROWS), pl.ds(z * LANES, LANES)] = value[z]
            for j in range(7):
                value = arrive_heat(warm_b, x, r, j)
                for z in range(2):
                    heat_out[j, x, pl.ds(r, ROWS), pl.ds(z * LANES, LANES)] = value[z]
            return carry

        lax.fori_loop(0, half, unit, 0)

        @pl.when(p == planes // 2)
        def _():
            for copy in column:
                copy.wait_recv()
            meet2[gx] = tree([meet[n] for n in range(ny)])
            for copy in sum_copies(meet2, 1, 0, gx, nx):
                copy.start()

        return carry

    lax.fori_loop(0, planes, third, 0)

    row = sum_copies(meet2, 1, 0, gx, nx)
    for copy in row:
        copy.wait_recv()
    flux_out[...] = tree([meet2[n] for n in range(nx)])

    for copy in column + row:
        copy.wait_send()
    for n, dx, dy in kind_list:
        inside(dy, kind_copy(n, dx, dy).wait_send)
    for turn, cold, warm in ((0, cold_a, warm_a), (1, cold_b, warm_b)):
        for dx, _ in FACES:
            wait_send_all(face_copies(turn, cold, warm, dx))()
        for dx, dy in CORNERS:
            inside(dy, wait_send_all([corner_copy(turn, cold, dx, dy)]))

        def drain(g, carry, turn=turn, cold=cold, warm=warm):
            for _, dy in SIDES:
                inside(dy, wait_send_all(side_copies(turn, cold, warm, dy, g)))
            return carry

        lax.fori_loop(0, groups, drain, 0)


def out_kernel(cells, flow_ref, heat_ref, flux_ref, flow_out, heat_out, total_out, sem):
    copies = [
        pltpu.make_async_copy(flow_ref, flow_out, sem.at[0]),
        pltpu.make_async_copy(heat_ref, heat_out, sem.at[1]),
    ]
    for copy in copies:
        copy.start()
    total_out[0, 0] = jnp.sum(flux_ref[...]) * (1.0 / cells)
    for copy in copies:
        copy.wait()


def per_device(nx, ny, flow, heat, kind):
    _, planes, height, length = flow.shape
    assert length == 2 * LANES and height % ROWS == 0 and planes % 4 == 0
    cold = (3, 3, 3, planes + 1, 2, height + ROWS, LANES)
    warm = (7, planes + 1, 2, height + ROWS, LANES)
    padded = (planes + 2, 2, height + 2 * ROWS, LANES)
    f32, i32 = jnp.float32, jnp.int32
    copies = 12 + 2 * 4 * (planes // 2)
    flow_new, heat_new, flux = pl.pallas_call(
        functools.partial(step_kernel, nx, ny),
        out_shape=(
            pltpu.VMEM(flow.shape, f32),
            pltpu.VMEM(heat.shape, f32),
            pltpu.VMEM((ROWS, LANES), f32),
        ),
        in_specs=[pl.BlockSpec(memory_space=pl.ANY)] * 3,
        out_specs=[pl.BlockSpec(memory_space=pltpu.VMEM)] * 3,
        scratch_shapes=[
            pltpu.VMEM(flow.shape, f32),
            pltpu.VMEM(heat.shape, f32),
            pltpu.VMEM(padded, i32),
            pltpu.VMEM(padded, i32),
            pltpu.VMEM((planes, 2, height, LANES), i32),
            pltpu.VMEM((6, planes, 2, height, LANES), f32),
            pltpu.VMEM(cold, f32),
            pltpu.VMEM(cold, f32),
            pltpu.VMEM(warm, f32),
            pltpu.VMEM(warm, f32),
            pltpu.VMEM((ny, ROWS, LANES), f32),
            pltpu.VMEM((nx, ROWS, LANES), f32),
            pltpu.VMEM((ROWS, LANES), f32),
            pltpu.SemaphoreType.DMA((2, planes)),
            pltpu.SemaphoreType.DMA((2,)),
            pltpu.SemaphoreType.DMA((2, copies)),
            pltpu.SemaphoreType.DMA((2, copies)),
            pltpu.SemaphoreType.DMA((8,)),
            pltpu.SemaphoreType.DMA((8,)),
            pltpu.SemaphoreType.DMA((2, max(nx, ny))),
            pltpu.SemaphoreType.DMA((2, max(nx, ny))),
        ],
        compiler_params=pltpu.CompilerParams(
            collective_id=0, has_side_effects=True, vmem_limit_bytes=50 * 1024 * 1024
        ),
    )(flow, heat, kind)
    cells = float(planes * nx * height * ny)
    flow_new, heat_new, total = pl.pallas_call(
        functools.partial(out_kernel, cells),
        out_shape=(
            jax.ShapeDtypeStruct(flow.shape, f32),
            jax.ShapeDtypeStruct(heat.shape, f32),
            jax.ShapeDtypeStruct((1, 1), f32),
        ),
        in_specs=[pl.BlockSpec(memory_space=pltpu.VMEM)] * 3,
        out_specs=[
            pl.BlockSpec(memory_space=pl.ANY),
            pl.BlockSpec(memory_space=pl.ANY),
            pl.BlockSpec(memory_space=pltpu.SMEM),
        ],
        scratch_shapes=[pltpu.SemaphoreType.DMA((2,))],
        compiler_params=pltpu.CompilerParams(vmem_limit_bytes=1024 * 1024),
    )(*[pltpu.with_memory_space_constraint(v, pltpu.VMEM) for v in (flow_new, heat_new, flux)])
    return flow_new, heat_new, total[0, 0]


def solution(mesh):
    return jax.shard_map(
        functools.partial(per_device, mesh.shape["gx"], mesh.shape["gy"]),
        mesh=mesh,
        in_specs=(P(None, "gx", "gy", None), P(None, "gx", "gy", None), P("gx", "gy", None)),
        out_specs=(P(None, "gx", "gy", None), P(None, "gx", "gy", None), P()),
        check_vma=False,
    )
```

```python
import functools

import jax
import jax.numpy as jnp
from jax import lax
from jax.experimental import pallas as pl
from jax.experimental.pallas import tpu as pltpu
from jax.sharding import PartitionSpec as P

MESH = pl.DeviceIdType.MESH
NEAR = 4
STEPS = 2
LANES = 128
ROWS = 8

PAIRS = [
    (a, b, e)
    for a in (-1, 0, 1)
    for b in (-1, 0, 1)
    for e in (-1, 0, 1)
    if (a, b, e) > (0, 0, 0)
]
HEAT_MOVES = [(0, 0, 0), (1, 0, 0), (-1, 0, 0), (0, 1, 0), (0, -1, 0), (0, 0, 1), (0, 0, -1)]
TAU_COOLANT = 0.5 + 4.0 * 0.05
TAU_METAL = 0.5 + 4.0 * 0.25
FACES = [(1, 0), (-1, 0)]
SIDES = [(0, 1), (0, -1)]
CORNERS = [(1, 1), (1, -1), (-1, 1), (-1, -1)]


def tree(terms):
    terms = list(terms)
    while len(terms) > 1:
        terms = [
            terms[k] + terms[k + 1] if k + 1 < len(terms) else terms[k]
            for k in range(0, len(terms), 2)
        ]
    return terms[0]


def signed(terms):
    plus = tree([value for sign, value in terms if sign > 0])
    minus = [value for sign, value in terms if sign < 0]
    return plus - tree(minus) if minus else plus


def inverse(value):
    guess = pl.reciprocal(value, approx=True)
    return guess * (2.0 - value * guess)


def lane_shift(pair, e, lane):
    if e == 0:
        return pair
    turned = [pltpu.roll(half, 1 if e == 1 else LANES - 1, 1) for half in pair]
    at_end = lane == (0 if e == 1 else LANES - 1)
    return [jnp.where(at_end, turned[1 - k], turned[k]) for k in range(2)]


def collide(rest, sums, diffs, heat, fluid):
    density = tree([rest] + sums)
    moments = [
        signed([(c[axis], diffs[k]) for k, c in enumerate(PAIRS) if c[axis] != 0])
        for axis in range(3)
    ]
    warmth = tree(heat)
    rate = inverse(0.5 + 0.15 * jnp.exp(0.5 - 0.5 * warmth))
    rate = jnp.where(fluid, rate, 0.0)
    scale = jnp.where(fluid, inverse(density) * 3.0, 0.0)
    vx, vy, vz = [moment * scale for moment in moments]
    keep = 0.5 - 0.5 * rate
    turn = jnp.where(fluid, keep, -0.5)
    weight = rate * density
    sx, sy, sz = (0.5 * vx) * vx, (0.5 * vy) * vy, (0.5 * vz) * vz
    total = sx + sy + sz
    base = 1.0 - total * (1.0 / 3.0)
    k1 = weight * (2.0 / 27.0)
    k2 = weight * (1.0 / 54.0)
    k3 = weight * (1.0 / 216.0)
    halves = {}
    speed = (vx, vy, vz)
    square = (sx, sy, sz)
    for axis in range(3):
        c = tuple(1 if n == axis else 0 for n in range(3))
        halves[c] = (k1 * (base + square[axis]), k1 * speed[axis])
    k2v = [k2 * v for v in speed]
    for m, n in ((0, 1), (0, 2), (1, 2)):
        even = k2 * (base + square[m] + square[n])
        cross = k2v[m] * speed[n]
        for sign in (1, -1):
            c = [0, 0, 0]
            c[m], c[n] = 1, sign
            halves[tuple(c)] = (
                (even + cross, k2v[m] + k2v[n]) if sign == 1 else (even - cross, k2v[m] - k2v[n])
            )
    k3v = [k3 * v for v in speed]
    even = k3 * (base + total)
    xy, xz, yz = k3v[0] * vy, k3v[0] * vz, k3v[1] * vz
    for b in (1, -1):
        outer = even + xy if b == 1 else even - xy
        inner = xz + yz if b == 1 else xz - yz
        slope = k3v[0] + k3v[1] if b == 1 else k3v[0] - k3v[1]
        for e in (1, -1):
            halves[(1, b, e)] = (
                (outer + inner, slope + k3v[2]) if e == 1 else (outer - inner, slope - k3v[2])
            )
    out_rest = (keep + keep) * rest + (weight * (8.0 / 27.0)) * base
    out_pairs = []
    for k, c in enumerate(PAIRS):
        even, odd = halves[c]
        even = keep * sums[k] + even
        odd = turn * diffs[k] + odd
        out_pairs.append((even + odd, even - odd))
    heat_rate = jnp.where(fluid, 1.0 / TAU_COOLANT, 1.0 / TAU_METAL)
    heat_keep = 1.0 - heat_rate
    part = (heat_rate * 0.125) * warmth
    slant = part * (4.0 / 3.0)
    hot = [heat_keep * heat[0] + (part + part)]
    for axis in range(3):
        lean = slant * speed[axis]
        hot.append(heat_keep * heat[1 + 2 * axis] + (part + lean))
        hot.append(heat_keep * heat[2 + 2 * axis] + (part - lean))
    return out_rest, out_pairs, hot


def step_kernel(
    nx, ny, flow_hbm, heat_hbm, kind_hbm, flow_buf, heat_buf, flux_out,
    kind, bits, weights, cold_a, cold_b, warm_a, warm_b, meet_column, meet_layer, flux_ref,
    in_sem, kind_sem, send_sem, recv_sem, kind_send, kind_recv, sum_send, sum_recv,
):
    gx, gy = lax.axis_index("gx"), lax.axis_index("gy")
    planes, height = flow_buf.shape[1], flow_buf.shape[2]
    lane = lax.broadcasted_iota(jnp.int32, (ROWS, LANES), 1)
    half = height // ROWS
    low_row, high_row = ROWS, ROWS + height - 1

    def outer_first(p):
        k = p // 2
        return lax.rem(p, 2) * (planes - 1 - k) + (1 - lax.rem(p, 2)) * k

    def outer_third(p):
        k = p // 2
        k = jnp.where(k < 3, lax.rem(k + 1, 3), k)
        return lax.rem(p, 2) * (planes - 1 - k) + (1 - lax.rem(p, 2)) * k

    def row_groups(p):
        low = lax.shift_right_logical(p, 6) * ROWS
        return [pl.multiple_of(low + h * ROWS, ROWS) for h in range(half)]

    def device(dx, dy):
        return (lax.rem(gx + dx + nx, nx), lax.rem(gy + dy + ny, ny))

    def inside(dy, act):
        if dy == 1:
            pl.when(gy < ny - 1)(act)
        elif dy == -1:
            pl.when(gy > 0)(act)
        else:
            act()

    kind_copies = [
        pltpu.make_async_copy(
            kind_hbm.at[:, :, pl.ds(z * LANES, LANES)],
            kind.at[pl.ds(1, planes), z, pl.ds(low_row, height), :],
            kind_sem.at[z],
        )
        for z in range(2)
    ]
    for copy in kind_copies:
        copy.start()

    def load(k):
        xs = pl.ds(2 * k, 2)
        return [
            pltpu.make_async_copy(flow_hbm.at[:, xs], flow_buf.at[:, xs], in_sem.at[0, k]),
            pltpu.make_async_copy(heat_hbm.at[:, xs], heat_buf.at[:, xs], in_sem.at[1, k]),
        ]

    for k in range(planes // 4):
        for copy in load(k) + load(planes // 2 - 1 - k):
            copy.start()

    along, across = gx // NEAR, lax.rem(gx, NEAR)
    far, near, core = gy // (2 * NEAR), lax.rem(gy, 2 * NEAR) // 2, lax.rem(gy, 2)
    fars = ny // (2 * NEAR)
    columns = 2 * fars * (nx // NEAR)
    layers = NEAR * NEAR
    column_index = (along * fars + far) * 2 + core
    layer_index = across * NEAR + near

    def column_device(d):
        n = lax.rem(column_index + d, columns)
        return ((n // (2 * fars)) * NEAR + across, (lax.rem(n, 2 * fars) // 2) * 2 * NEAR + near * 2 + lax.rem(n, 2))

    def layer_device(d):
        n = lax.rem(layer_index + d, layers)
        return (along * NEAR + n // NEAR, far * 2 * NEAR + lax.rem(n, NEAR) * 2 + core)

    barrier = pltpu.get_barrier_semaphore()
    greeted = [device(dx, dy) for dx, dy in FACES + SIDES + CORNERS]
    greeted += [column_device(d) for d in range(1, columns)]
    greeted += [layer_device(d) for d in range(1, layers)]
    for target in greeted:
        pl.semaphore_signal(barrier, inc=1, device_id=target, device_id_type=MESH)

    for copy in kind_copies:
        copy.wait()

    def spans(dx, dy, xs):
        src_x = {1: pl.ds(planes, 1), -1: pl.ds(1, 1), 0: xs}[dx]
        dst_x = {1: pl.ds(0, 1), -1: pl.ds(planes + 1, 1), 0: xs}[dx]
        src_y = {1: pl.ds(high_row, 1), -1: pl.ds(low_row, 1), 0: pl.ds(low_row, height)}[dy]
        dst_y = {1: pl.ds(low_row - 1, 1), -1: pl.ds(high_row + 1, 1), 0: pl.ds(low_row, height)}[dy]
        return (src_x, src_y), (dst_x, dst_y)

    def remote(src, dst, send, recv, dx, dy):
        return pltpu.make_async_remote_copy(
            src_ref=src, dst_ref=dst, send_sem=send, recv_sem=recv,
            device_id=device(dx, dy), device_id_type=MESH,
        )

    every = pl.ds(1, planes)

    def kind_copy(n, dx, dy):
        (sx, sy), (tx, ty) = spans(dx, dy, every)
        return remote(
            kind.at[sx, :, sy, :], kind.at[tx, :, ty, :], kind_send.at[n], kind_recv.at[n], dx, dy
        )

    kind_list = [(n, dx, dy) for n, (dx, dy) in enumerate(FACES + SIDES + CORNERS)]

    def moving(cold, dx, dy, xs, ys):
        a = dx + 1 if dx else slice(None)
        b = dy + 1 if dy else slice(None)
        return cold.at[a, b, :, xs, :, ys, :]

    def flow_copy(turn, cold, dx, dy, send, recv, xs=every):
        (sx, sy), (tx, ty) = spans(dx, dy, xs)
        return remote(
            moving(cold, dx, dy, sx, sy), moving(cold, dx, dy, tx, ty),
            send_sem.at[turn, send], recv_sem.at[turn, recv], dx, dy,
        )

    def heat_copy(turn, warm, dx, dy, send, recv, xs=every):
        j = HEAT_MOVES.index((dx, dy, 0))
        (sx, sy), (tx, ty) = spans(dx, dy, xs)
        return remote(
            warm.at[j, sx, :, sy, :], warm.at[j, tx, :, ty, :],
            send_sem.at[turn, send], recv_sem.at[turn, recv], dx, dy,
        )

    def face_copies(turn, cold, warm, n):
        dx, _ = FACES[n]
        return [
            flow_copy(turn, cold, dx, 0, 2 * n, 2 * n),
            heat_copy(turn, warm, dx, 0, 2 * n + 1, 2 * n + 1),
        ]

    def corner_copy(turn, cold, n):
        dx, dy = CORNERS[n]
        return flow_copy(turn, cold, dx, dy, 4 + n, 4 + n)

    group = planes // 4

    def side_copies(turn, cold, warm, n, g=None):
        _, dy = SIDES[n]
        xs = every if g is None else pl.ds(1 + group * g, group)
        recv = 8 + 2 * (4 * n + (0 if g is None else g))
        return [
            flow_copy(turn, cold, 0, dy, 8 + 2 * n, recv, xs),
            heat_copy(turn, warm, 0, dy, 9 + 2 * n, recv + 1, xs),
        ]

    def each(copies, what):
        def act():
            for copy in copies:
                getattr(copy, what)()
        return act

    def faces(turn, cold, warm, what):
        sign = -1 if what == "wait_recv" else 1
        for n in range(2):
            each(face_copies(turn, cold, warm, n), what)()
        for n in range(4):
            inside(sign * CORNERS[n][1], each([corner_copy(turn, cold, n)], what))

    def sides(turn, cold, warm, gs, what):
        sign = -1 if what == "wait_recv" else 1
        for n in range(2):
            copies = [c for g in gs for c in side_copies(turn, cold, warm, n, g)]
            inside(sign * SIDES[n][1], each(copies, what))

    def store(cold, warm, x, r, z, rest, pairs, hot):
        def at(value, target, c):
            target[c + (x + 1, z, pl.ds(r + ROWS, ROWS), slice(None))] = value
        at(rest, cold, (1, 1, 1))
        for (a, b, e), (ahead, back) in zip(PAIRS, pairs):
            at(ahead, cold, (1 + a, 1 + b, 1 + e))
            at(back, cold, (1 - a, 1 - b, 1 - e))
        for j in range(7):
            at(hot[j], warm, (j,))

    def wall_rows(warm, x):
        @pl.when(gy == 0)
        def _():
            for z in range(2):
                warm[3, x + 1, z, pl.ds(low_row - 1, 1), :] = warm[4, x + 1, z, pl.ds(low_row, 1), :]

        @pl.when(gy == ny - 1)
        def _():
            for z in range(2):
                warm[4, x + 1, z, pl.ds(high_row + 1, 1), :] = warm[3, x + 1, z, pl.ds(high_row, 1), :]

    def outside_rows(row):
        def act():
            kind[:, :, pl.ds(row, 1), :] = jnp.full((planes + 2, 2, 1, LANES), 2, jnp.int32)
        return act

    together = 2

    def mask(q, carry):
        for x in [q * together + n for n in range(together)]:
            for r in row_groups(q):
                own = [kind[x + 1, z, pl.ds(r + ROWS, ROWS), :] for z in range(2)]
                lines, near = [], []
                for z in range(2):
                    found = {}
                    for a in (-1, 0, 1):
                        for b in (-1, 0, 1):
                            value = own[z] if a == b == 0 else kind[x + 1 - a, z, pl.ds(r + ROWS - b, ROWS), :]
                            found[a, b] = value
                    near.append([found[-1, 0], found[1, 0], found[0, -1], found[0, 1]])
                    lines.append(tree([
                        jnp.where(found[a, b] == 0, 1 << (9 * (a + 1) + 3 * (b + 1)), 0)
                        for a in (-1, 0, 1) for b in (-1, 0, 1)
                    ]))
                above = lane_shift(lines, -1, lane)
                below = lane_shift(lines, 1, lane)
                for z in range(2):
                    code = above[z] + (lines[z] << 1) + (below[z] << 2)
                    bits[x, z, pl.ds(r, ROWS), :] = jnp.where(own[z] == 0, code, 0)
                    others = [jnp.where(v == 2, own[z], v) for v in near[z]]
                    others += [1 - ((v[z] >> 12) & 1) for v in (above, below)]
                    for j in range(6):
                        weights[j, x, z, pl.ds(r, ROWS), :] = (own[z] - others[j]).astype(jnp.float32)
        return carry

    def first(p, carry):
        x = outer_first(p)

        @pl.when(lax.rem(p, 4) < 2)
        def _():
            for copy in load(x // 2):
                copy.wait()

        @pl.when(p == 1)
        def _():
            pl.semaphore_wait(barrier, len(greeted))
            for n, dx, dy in kind_list:
                inside(dy, kind_copy(n, dx, dy).start)

        for r in row_groups(p):
            for z in range(2):
                at = (x, pl.ds(r, ROWS), pl.ds(z * LANES, LANES))
                values = [flow_buf[(i,) + at] for i in range(27)]
                heat = [heat_buf[(j,) + at] for j in range(7)]
                fluid = kind[x + 1, z, pl.ds(r + ROWS, ROWS), :] == 0
                sums = [values[i] + values[26 - i] for i in range(14, 27)]
                diffs = [values[i] - values[26 - i] for i in range(14, 27)]
                rest, pairs, hot = collide(values[13], sums, diffs, heat, fluid)
                store(cold_a, warm_a, x, r, z, rest, pairs, hot)
        wall_rows(warm_a, x)

        @pl.when(p == 1)
        def _():
            faces(0, cold_a, warm_a, "start")

        @pl.when(p == planes // 2 - 1)
        def _():
            sides(0, cold_a, warm_a, (0, 3), "start")

        return carry

    lax.fori_loop(0, planes, first, 0)
    sides(0, cold_a, warm_a, (1, 2), "start")

    for n, dx, dy in kind_list:
        inside(-dy, kind_copy(n, dx, dy).wait_recv)
    pl.when(gy == 0)(outside_rows(low_row - 1))
    pl.when(gy == ny - 1)(outside_rows(high_row + 1))
    lax.fori_loop(0, planes // together, mask, 0)

    def arrive(cold, x, r, code, c):
        a, b, e = c
        number = 9 * (a + 1) + 3 * (b + 1) + (e + 1)
        found = lane_shift(
            [cold[a + 1, b + 1, e + 1, x + 1 - a, z, pl.ds(r + ROWS - b, ROWS), :] for z in range(2)],
            e, lane,
        )
        return [
            jnp.where(
                (code[z] & (1 << number)) != 0,
                found[z],
                cold[1 - a, 1 - b, 1 - e, x + 1, z, pl.ds(r + ROWS, ROWS), :],
            )
            for z in range(2)
        ]

    def arrive_heat(warm, x, r, j):
        a, b, e = HEAT_MOVES[j]
        found = [warm[j, x + 1 - a, z, pl.ds(r + ROWS - b, ROWS), :] for z in range(2)]
        return lane_shift(found, e, lane)

    def takes_before(p, turn, cold, warm):
        @pl.when(p == 0)
        def _():
            sides(turn, cold, warm, (0, 3), "wait_recv")

        @pl.when(p == 4)
        def _():
            faces(turn, cold, warm, "wait_recv")

        @pl.when(p == 6)
        def _():
            sides(turn, cold, warm, (1, 2), "wait_recv")

    flux_ref[...] = jnp.zeros_like(flux_ref)

    def second(p, carry):
        x = outer_third(p)
        takes_before(p, 0, cold_a, warm_a)
        flux = flux_ref[...]
        for r in row_groups(p):
            code = [bits[x, z, pl.ds(r, ROWS), :] for z in range(2)]
            rest = [cold_a[1, 1, 1, x + 1, z, pl.ds(r + ROWS, ROWS), :] for z in range(2)]
            sums, diffs = [], []
            for a, b, e in PAIRS:
                ahead = arrive(cold_a, x, r, code, (a, b, e))
                back = arrive(cold_a, x, r, code, (-a, -b, -e))
                sums.append([ahead[z] + back[z] for z in range(2)])
                diffs.append([ahead[z] - back[z] for z in range(2)])
            heat = [arrive_heat(warm_a, x, r, j) for j in range(7)]
            for z in range(2):
                fluid = kind[x + 1, z, pl.ds(r + ROWS, ROWS), :] == 0
                out_rest, pairs, hot = collide(
                    rest[z], [s[z] for s in sums], [d[z] for d in diffs], [g[z] for g in heat], fluid
                )
                store(cold_b, warm_b, x, r, z, out_rest, pairs, hot)
                terms = []
                for j in range(1, 7):
                    was = warm_a[j, x + 1, z, pl.ds(r + ROWS, ROWS), :]
                    terms.append(weights[j - 1, x, z, pl.ds(r, ROWS), :] * (was + hot[j]))
                flux = flux + tree(terms)
        flux_ref[...] = flux
        wall_rows(warm_b, x)

        @pl.when(p == 5)
        def _():
            faces(1, cold_b, warm_b, "start")

        @pl.when(p == planes // 2 - 1)
        def _():
            sides(1, cold_b, warm_b, (0, 3), "start")

        return carry

    lax.fori_loop(0, planes, second, 0)

    def sum_copy(slots, stage, at, target):
        return pltpu.make_async_remote_copy(
            src_ref=slots.at[at], dst_ref=slots.at[at],
            send_sem=sum_send.at[stage], recv_sem=sum_recv.at[stage],
            device_id=target, device_id_type=MESH,
        )

    def column_all():
        return sum_copy(meet_column, 0, pl.ds(0, columns - 1), column_device(1))

    def layer_all():
        return sum_copy(meet_layer, 1, pl.ds(0, layers - 1), layer_device(1))

    meet_column[column_index] = flux_ref[...]
    for d in range(1, columns):
        sum_copy(meet_column, 0, column_index, column_device(d)).start()
    sides(1, cold_b, warm_b, (1, 2), "start")

    def third(p, carry):
        x = outer_third(p)

        @pl.when(p == 6)
        def _():
            column_all().wait_recv()
            meet_layer[layer_index] = tree([meet_column[n] for n in range(columns)])
            for d in range(1, layers):
                sum_copy(meet_layer, 1, layer_index, layer_device(d)).start()

        takes_before(p, 1, cold_b, warm_b)
        for r in row_groups(p):
            code = [bits[x, z, pl.ds(r, ROWS), :] for z in range(2)]
            for a in (-1, 0, 1):
                for b in (-1, 0, 1):
                    for e in (-1, 0, 1):
                        i = 9 * (a + 1) + 3 * (b + 1) + (e + 1)
                        if i == 13:
                            value = [cold_b[1, 1, 1, x + 1, z, pl.ds(r + ROWS, ROWS), :] for z in range(2)]
                        else:
                            value = arrive(cold_b, x, r, code, (a, b, e))
                        for z in range(2):
                            flow_buf[i, x, pl.ds(r, ROWS), pl.ds(z * LANES, LANES)] = value[z]
            for j in range(7):
                value = arrive_heat(warm_b, x, r, j)
                for z in range(2):
                    heat_buf[j, x, pl.ds(r, ROWS), pl.ds(z * LANES, LANES)] = value[z]

        return carry

    lax.fori_loop(0, planes, third, 0)

    layer_all().wait_recv()
    flux_out[...] = tree([meet_layer[n] for n in range(layers)])

    column_all().wait_send()
    layer_all().wait_send()
    for n, dx, dy in kind_list:
        inside(dy, kind_copy(n, dx, dy).wait_send)
    for turn, cold, warm in ((0, cold_a, warm_a), (1, cold_b, warm_b)):
        faces(turn, cold, warm, "wait_send")
        sides(turn, cold, warm, (None,), "wait_send")


def out_kernel(cells, flow_ref, heat_ref, flux_ref, flow_out, heat_out, total_out, sem):
    copies = [
        pltpu.make_async_copy(flow_ref, flow_out, sem.at[0]),
        pltpu.make_async_copy(heat_ref, heat_out, sem.at[1]),
    ]
    for copy in copies:
        copy.start()
    total_out[0, 0] = jnp.sum(flux_ref[...]) * (1.0 / cells)
    for copy in copies:
        copy.wait()


def per_device(nx, ny, flow, heat, kind):
    _, planes, height, length = flow.shape
    assert length == 2 * LANES and height % ROWS == 0 and planes == 16
    assert nx % NEAR == 0 and ny % (2 * NEAR) == 0
    padded = (planes + 2, 2, height + 2 * ROWS, LANES)
    cold, warm = (3, 3, 3) + padded, (7,) + padded
    f32, i32 = jnp.float32, jnp.int32
    flow_new, heat_new, flux = pl.pallas_call(
        functools.partial(step_kernel, nx, ny),
        out_shape=(
            pltpu.VMEM(flow.shape, f32),
            pltpu.VMEM(heat.shape, f32),
            pltpu.VMEM((ROWS, LANES), f32),
        ),
        in_specs=[pl.BlockSpec(memory_space=pl.ANY)] * 3,
        out_specs=[pl.BlockSpec(memory_space=pltpu.VMEM)] * 3,
        scratch_shapes=[
            pltpu.VMEM(padded, i32),
            pltpu.VMEM((planes, 2, height, LANES), i32),
            pltpu.VMEM((6, planes, 2, height, LANES), f32),
            pltpu.VMEM(cold, f32),
            pltpu.VMEM(cold, f32),
            pltpu.VMEM(warm, f32),
            pltpu.VMEM(warm, f32),
            pltpu.VMEM((nx * ny // (NEAR * NEAR), ROWS, LANES), f32),
            pltpu.VMEM((NEAR * NEAR, ROWS, LANES), f32),
            pltpu.VMEM((ROWS, LANES), f32),
            pltpu.SemaphoreType.DMA((2, planes // 2)),
            pltpu.SemaphoreType.DMA((2,)),
            pltpu.SemaphoreType.DMA((2, 12)),
            pltpu.SemaphoreType.DMA((2, 24)),
            pltpu.SemaphoreType.DMA((8,)),
            pltpu.SemaphoreType.DMA((8,)),
            pltpu.SemaphoreType.DMA((2,)),
            pltpu.SemaphoreType.DMA((2,)),
        ],
        compiler_params=pltpu.CompilerParams(
            collective_id=0, has_side_effects=True, vmem_limit_bytes=44 * 1024 * 1024
        ),
    )(*[pltpu.with_memory_space_constraint(v, pltpu.HBM) for v in (flow, heat, kind)])
    cells = float(planes * nx * height * ny)
    flow_new, heat_new, total = pl.pallas_call(
        functools.partial(out_kernel, cells),
        out_shape=(
            jax.ShapeDtypeStruct(flow.shape, f32),
            jax.ShapeDtypeStruct(heat.shape, f32),
            jax.ShapeDtypeStruct((1, 1), f32),
        ),
        in_specs=[pl.BlockSpec(memory_space=pltpu.VMEM)] * 3,
        out_specs=[
            pl.BlockSpec(memory_space=pl.ANY),
            pl.BlockSpec(memory_space=pl.ANY),
            pl.BlockSpec(memory_space=pltpu.SMEM),
        ],
        scratch_shapes=[pltpu.SemaphoreType.DMA((2,))],
        compiler_params=pltpu.CompilerParams(vmem_limit_bytes=1024 * 1024),
    )(*[pltpu.with_memory_space_constraint(v, pltpu.VMEM) for v in (flow_new, heat_new, flux)])
    return flow_new, heat_new, total[0, 0]


def solution(mesh):
    return jax.shard_map(
        functools.partial(per_device, mesh.shape["gx"], mesh.shape["gy"]),
        mesh=mesh,
        in_specs=(P(None, "gx", "gy", None), P(None, "gx", "gy", None), P("gx", "gy", None)),
        out_specs=(P(None, "gx", "gy", None), P(None, "gx", "gy", None), P()),
        check_vma=False,
    )
```

```python
import functools

import jax
import jax.numpy as jnp
from jax import lax
from jax.experimental import pallas as pl
from jax.experimental.pallas import tpu as pltpu
from jax.sharding import PartitionSpec as P

MESH = pl.DeviceIdType.MESH
NEAR = 4
STEPS = 2
LANES = 128
ROWS = 8

PAIRS = [
    (a, b, e)
    for a in (-1, 0, 1)
    for b in (-1, 0, 1)
    for e in (-1, 0, 1)
    if (a, b, e) > (0, 0, 0)
]
HEAT_MOVES = [(0, 0, 0), (1, 0, 0), (-1, 0, 0), (0, 1, 0), (0, -1, 0), (0, 0, 1), (0, 0, -1)]
TAU_COOLANT = 0.5 + 4.0 * 0.05
TAU_METAL = 0.5 + 4.0 * 0.25
FACES = [(1, 0), (-1, 0)]
SIDES = [(0, 1), (0, -1)]
CORNERS = [(1, 1), (1, -1), (-1, 1), (-1, -1)]


def tree(terms):
    terms = list(terms)
    while len(terms) > 1:
        terms = [
            terms[k] + terms[k + 1] if k + 1 < len(terms) else terms[k]
            for k in range(0, len(terms), 2)
        ]
    return terms[0]


def signed(terms):
    plus = tree([value for sign, value in terms if sign > 0])
    minus = [value for sign, value in terms if sign < 0]
    return plus - tree(minus) if minus else plus


def inverse(value):
    guess = pl.reciprocal(value, approx=True)
    return guess * (2.0 - value * guess)


def lane_shift(pair, e, lane):
    if e == 0:
        return pair
    turned = [pltpu.roll(half, 1 if e == 1 else LANES - 1, 1) for half in pair]
    at_end = lane == (0 if e == 1 else LANES - 1)
    return [jnp.where(at_end, turned[1 - k], turned[k]) for k in range(2)]


def collide(rest, sums, diffs, heat, fluid):
    density = tree([rest] + sums)
    moments = [
        signed([(c[axis], diffs[k]) for k, c in enumerate(PAIRS) if c[axis] != 0])
        for axis in range(3)
    ]
    warmth = tree(heat)
    rate = inverse(0.5 + 0.15 * jnp.exp(0.5 - 0.5 * warmth))
    rate = jnp.where(fluid, rate, 0.0)
    scale = jnp.where(fluid, inverse(density) * 3.0, 0.0)
    vx, vy, vz = [moment * scale for moment in moments]
    keep = 0.5 - 0.5 * rate
    turn = jnp.where(fluid, keep, -0.5)
    weight = rate * density
    sx, sy, sz = (0.5 * vx) * vx, (0.5 * vy) * vy, (0.5 * vz) * vz
    total = sx + sy + sz
    base = 1.0 - total * (1.0 / 3.0)
    k1 = weight * (2.0 / 27.0)
    k2 = weight * (1.0 / 54.0)
    k3 = weight * (1.0 / 216.0)
    halves = {}
    speed = (vx, vy, vz)
    square = (sx, sy, sz)
    for axis in range(3):
        c = tuple(1 if n == axis else 0 for n in range(3))
        halves[c] = (k1 * (base + square[axis]), k1 * speed[axis])
    k2v = [k2 * v for v in speed]
    for m, n in ((0, 1), (0, 2), (1, 2)):
        even = k2 * (base + square[m] + square[n])
        cross = k2v[m] * speed[n]
        for sign in (1, -1):
            c = [0, 0, 0]
            c[m], c[n] = 1, sign
            halves[tuple(c)] = (
                (even + cross, k2v[m] + k2v[n]) if sign == 1 else (even - cross, k2v[m] - k2v[n])
            )
    k3v = [k3 * v for v in speed]
    even = k3 * (base + total)
    xy, xz, yz = k3v[0] * vy, k3v[0] * vz, k3v[1] * vz
    for b in (1, -1):
        outer = even + xy if b == 1 else even - xy
        inner = xz + yz if b == 1 else xz - yz
        slope = k3v[0] + k3v[1] if b == 1 else k3v[0] - k3v[1]
        for e in (1, -1):
            halves[(1, b, e)] = (
                (outer + inner, slope + k3v[2]) if e == 1 else (outer - inner, slope - k3v[2])
            )
    out_rest = (keep + keep) * rest + (weight * (8.0 / 27.0)) * base
    out_pairs = []
    for k, c in enumerate(PAIRS):
        even, odd = halves[c]
        even = keep * sums[k] + even
        odd = turn * diffs[k] + odd
        out_pairs.append((even + odd, even - odd))
    heat_rate = jnp.where(fluid, 1.0 / TAU_COOLANT, 1.0 / TAU_METAL)
    heat_keep = 1.0 - heat_rate
    part = (heat_rate * 0.125) * warmth
    slant = part * (4.0 / 3.0)
    hot = [heat_keep * heat[0] + (part + part)]
    for axis in range(3):
        lean = slant * speed[axis]
        hot.append(heat_keep * heat[1 + 2 * axis] + (part + lean))
        hot.append(heat_keep * heat[2 + 2 * axis] + (part - lean))
    return out_rest, out_pairs, hot


def step_kernel(
    nx, ny, flow_hbm, heat_hbm, kind_hbm, flow_buf, heat_buf, flux_out,
    kind, bits, weights, cold_a, cold_b, warm_a, warm_b, meet_column, meet_layer, flux_ref,
    in_sem, kind_sem, send_sem, recv_sem, kind_send, kind_recv, sum_send, sum_recv,
):
    gx, gy = lax.axis_index("gx"), lax.axis_index("gy")
    planes, height = flow_buf.shape[1], flow_buf.shape[2]
    lane = lax.broadcasted_iota(jnp.int32, (ROWS, LANES), 1)
    half = height // ROWS
    low_row, high_row = ROWS, ROWS + height - 1

    def outer_first(p):
        k = p // 2
        return lax.rem(p, 2) * (planes - 1 - k) + (1 - lax.rem(p, 2)) * k

    def outer_third(p):
        k = p // 2
        k = jnp.where(k < 3, lax.rem(k + 1, 3), k)
        return lax.rem(p, 2) * (planes - 1 - k) + (1 - lax.rem(p, 2)) * k

    def row_groups(p):
        low = lax.shift_right_logical(p, 6) * ROWS
        return [pl.multiple_of(low + h * ROWS, ROWS) for h in range(half)]

    def device(dx, dy):
        return (lax.rem(gx + dx + nx, nx), lax.rem(gy + dy + ny, ny))

    def inside(dy, act):
        if dy == 1:
            pl.when(gy < ny - 1)(act)
        elif dy == -1:
            pl.when(gy > 0)(act)
        else:
            act()

    along, across = gx // NEAR, lax.rem(gx, NEAR)
    far, near, core = gy // (2 * NEAR), lax.rem(gy, 2 * NEAR) // 2, lax.rem(gy, 2)
    fars = ny // (2 * NEAR)
    columns = 2 * fars * (nx // NEAR)
    layers = NEAR * NEAR
    column_index = (along * fars + far) * 2 + core
    layer_index = across * NEAR + near

    def column_device(d):
        n = lax.rem(column_index + d, columns)
        return ((n // (2 * fars)) * NEAR + across, (lax.rem(n, 2 * fars) // 2) * 2 * NEAR + near * 2 + lax.rem(n, 2))

    def layer_device(d):
        n = lax.rem(layer_index + d, layers)
        return (along * NEAR + n // NEAR, far * 2 * NEAR + lax.rem(n, NEAR) * 2 + core)

    barrier = pltpu.get_barrier_semaphore()
    greeted = [device(dx, dy) for dx, dy in FACES + SIDES + CORNERS]
    greeted += [column_device(d) for d in range(1, columns)]
    greeted += [layer_device(d) for d in range(1, layers)]
    for target in greeted:
        pl.semaphore_signal(barrier, inc=1, device_id=target, device_id_type=MESH)

    kind_copies = [
        pltpu.make_async_copy(
            kind_hbm.at[:, :, pl.ds(z * LANES, LANES)],
            kind.at[pl.ds(1, planes), z, pl.ds(low_row, height), :],
            kind_sem.at[z],
        )
        for z in range(2)
    ]
    for copy in kind_copies:
        copy.start()

    def load(k):
        xs = pl.ds(2 * k, 2)
        return [
            pltpu.make_async_copy(flow_hbm.at[:, xs], flow_buf.at[:, xs], in_sem.at[0, k]),
            pltpu.make_async_copy(heat_hbm.at[:, xs], heat_buf.at[:, xs], in_sem.at[1, k]),
        ]

    for k in range(planes // 4):
        for copy in load(k) + load(planes // 2 - 1 - k):
            copy.start()

    for copy in kind_copies:
        copy.wait()

    def spans(dx, dy, xs):
        src_x = {1: pl.ds(planes, 1), -1: pl.ds(1, 1), 0: xs}[dx]
        dst_x = {1: pl.ds(0, 1), -1: pl.ds(planes + 1, 1), 0: xs}[dx]
        src_y = {1: pl.ds(high_row, 1), -1: pl.ds(low_row, 1), 0: pl.ds(low_row, height)}[dy]
        dst_y = {1: pl.ds(low_row - 1, 1), -1: pl.ds(high_row + 1, 1), 0: pl.ds(low_row, height)}[dy]
        return (src_x, src_y), (dst_x, dst_y)

    def remote(src, dst, send, recv, dx, dy):
        return pltpu.make_async_remote_copy(
            src_ref=src, dst_ref=dst, send_sem=send, recv_sem=recv,
            device_id=device(dx, dy), device_id_type=MESH,
        )

    every = pl.ds(1, planes)

    def kind_copy(n, dx, dy):
        (sx, sy), (tx, ty) = spans(dx, dy, every)
        return remote(
            kind.at[sx, :, sy, :], kind.at[tx, :, ty, :], kind_send.at[n], kind_recv.at[n], dx, dy
        )

    kind_list = [(n, dx, dy) for n, (dx, dy) in enumerate(FACES + SIDES + CORNERS)]

    def moving(cold, dx, dy, xs, ys):
        a = dx + 1 if dx else slice(None)
        b = dy + 1 if dy else slice(None)
        return cold.at[a, b, :, xs, :, ys, :]

    def flow_copy(turn, cold, dx, dy, send, recv, xs=every):
        (sx, sy), (tx, ty) = spans(dx, dy, xs)
        return remote(
            moving(cold, dx, dy, sx, sy), moving(cold, dx, dy, tx, ty),
            send_sem.at[turn, send], recv_sem.at[turn, recv], dx, dy,
        )

    def heat_copy(turn, warm, dx, dy, send, recv, xs=every):
        j = HEAT_MOVES.index((dx, dy, 0))
        (sx, sy), (tx, ty) = spans(dx, dy, xs)
        return remote(
            warm.at[j, sx, :, sy, :], warm.at[j, tx, :, ty, :],
            send_sem.at[turn, send], recv_sem.at[turn, recv], dx, dy,
        )

    def face_copies(turn, cold, warm, n):
        dx, _ = FACES[n]
        return [
            flow_copy(turn, cold, dx, 0, 2 * n, 2 * n),
            heat_copy(turn, warm, dx, 0, 2 * n + 1, 2 * n + 1),
        ]

    def corner_copy(turn, cold, n):
        dx, dy = CORNERS[n]
        return flow_copy(turn, cold, dx, dy, 4 + n, 4 + n)

    group = planes // 4

    def side_copies(turn, cold, warm, n, g=None):
        _, dy = SIDES[n]
        xs = every if g is None else pl.ds(1 + group * g, group)
        recv = 8 + 2 * (4 * n + (0 if g is None else g))
        return [
            flow_copy(turn, cold, 0, dy, 8 + 2 * n, recv, xs),
            heat_copy(turn, warm, 0, dy, 9 + 2 * n, recv + 1, xs),
        ]

    def each(copies, what):
        def act():
            for copy in copies:
                getattr(copy, what)()
        return act

    def faces(turn, cold, warm, what):
        sign = -1 if what == "wait_recv" else 1
        for n in range(2):
            each(face_copies(turn, cold, warm, n), what)()
        for n in range(4):
            inside(sign * CORNERS[n][1], each([corner_copy(turn, cold, n)], what))

    def sides(turn, cold, warm, gs, what):
        sign = -1 if what == "wait_recv" else 1
        for n in range(2):
            copies = [c for g in gs for c in side_copies(turn, cold, warm, n, g)]
            inside(sign * SIDES[n][1], each(copies, what))

    def own(x, r, z):
        return (x + 1, z, pl.ds(r + ROWS, ROWS), slice(None))

    def store_flow(cold, x, r, z, rest, pairs):
        here = own(x, r, z)
        cold[(1, 1, 1) + here] = rest
        for (a, b, e), (ahead, back) in zip(PAIRS, pairs):
            cold[(1 + a, 1 + b, 1 + e) + here] = ahead
            cold[(1 - a, 1 - b, 1 - e) + here] = back

    def store_heat(warm, x, r, z, hot):
        for j in range(7):
            warm[(j,) + own(x, r, z)] = hot[j]

    def wall_rows(warm, x):
        @pl.when(gy == 0)
        def _():
            for z in range(2):
                warm[3, x + 1, z, pl.ds(low_row - 1, 1), :] = warm[4, x + 1, z, pl.ds(low_row, 1), :]

        @pl.when(gy == ny - 1)
        def _():
            for z in range(2):
                warm[4, x + 1, z, pl.ds(high_row + 1, 1), :] = warm[3, x + 1, z, pl.ds(high_row, 1), :]

    def outside_rows(row):
        def act():
            kind[:, :, pl.ds(row, 1), :] = jnp.full((planes + 2, 2, 1, LANES), 2, jnp.int32)
        return act

    together = 2

    def mask(q, carry):
        for x in [q * together + n for n in range(together)]:
            for r in row_groups(q):
                own = [kind[x + 1, z, pl.ds(r + ROWS, ROWS), :] for z in range(2)]
                lines, near = [], []
                for z in range(2):
                    found = {}
                    for a in (-1, 0, 1):
                        for b in (-1, 0, 1):
                            value = own[z] if a == b == 0 else kind[x + 1 - a, z, pl.ds(r + ROWS - b, ROWS), :]
                            found[a, b] = value
                    near.append([found[-1, 0], found[1, 0], found[0, -1], found[0, 1]])
                    lines.append(tree([
                        jnp.where(found[a, b] == 0, 1 << (9 * (a + 1) + 3 * (b + 1)), 0)
                        for a in (-1, 0, 1) for b in (-1, 0, 1)
                    ]))
                above = lane_shift(lines, -1, lane)
                below = lane_shift(lines, 1, lane)
                for z in range(2):
                    code = above[z] + (lines[z] << 1) + (below[z] << 2)
                    bits[x, z, pl.ds(r, ROWS), :] = jnp.where(own[z] == 0, code, 0)
                    others = [jnp.where(v == 2, own[z], v) for v in near[z]]
                    others += [1 - ((v[z] >> 12) & 1) for v in (above, below)]
                    for j in range(6):
                        weights[j, x, z, pl.ds(r, ROWS), :] = (own[z] - others[j]).astype(jnp.float32)
        return carry

    def first(p, carry):
        x = outer_first(p)

        @pl.when(lax.rem(p, 4) < 2)
        def _():
            for copy in load(x // 2):
                copy.wait()

        @pl.when(p == 3)
        def _():
            pl.semaphore_wait(barrier, len(greeted))
            for n, dx, dy in kind_list:
                inside(dy, kind_copy(n, dx, dy).start)

        for r in row_groups(p):
            for z in range(2):
                at = (x, pl.ds(r, ROWS), pl.ds(z * LANES, LANES))
                values = [flow_buf[(i,) + at] for i in range(27)]
                heat = [heat_buf[(j,) + at] for j in range(7)]
                fluid = kind[x + 1, z, pl.ds(r + ROWS, ROWS), :] == 0
                sums = [values[i] + values[26 - i] for i in range(14, 27)]
                diffs = [values[i] - values[26 - i] for i in range(14, 27)]
                rest, pairs, hot = collide(values[13], sums, diffs, heat, fluid)
                store_flow(cold_a, x, r, z, rest, pairs)
                store_heat(warm_a, x, r, z, hot)
        wall_rows(warm_a, x)

        @pl.when(p == 3)
        def _():
            faces(0, cold_a, warm_a, "start")

        @pl.when(p == planes // 2 - 1)
        def _():
            sides(0, cold_a, warm_a, (0, 3), "start")

        return carry

    lax.fori_loop(0, planes, first, 0)
    sides(0, cold_a, warm_a, (1, 2), "start")

    for n, dx, dy in kind_list:
        inside(-dy, kind_copy(n, dx, dy).wait_recv)
    pl.when(gy == 0)(outside_rows(low_row - 1))
    pl.when(gy == ny - 1)(outside_rows(high_row + 1))
    lax.fori_loop(0, planes // together, mask, 0)

    def arrive(cold, x, r, code, c):
        a, b, e = c
        number = 9 * (a + 1) + 3 * (b + 1) + (e + 1)
        found = lane_shift(
            [cold[a + 1, b + 1, e + 1, x + 1 - a, z, pl.ds(r + ROWS - b, ROWS), :] for z in range(2)],
            e, lane,
        )
        return [
            jnp.where(
                (code[z] & (1 << number)) != 0,
                found[z],
                cold[1 - a, 1 - b, 1 - e, x + 1, z, pl.ds(r + ROWS, ROWS), :],
            )
            for z in range(2)
        ]

    def arrive_heat(warm, x, r, j):
        a, b, e = HEAT_MOVES[j]
        found = [warm[j, x + 1 - a, z, pl.ds(r + ROWS - b, ROWS), :] for z in range(2)]
        return lane_shift(found, e, lane)

    def takes_before(p, turn, cold, warm):
        @pl.when(p == 0)
        def _():
            sides(turn, cold, warm, (0, 3), "wait_recv")

        @pl.when(p == 4)
        def _():
            faces(turn, cold, warm, "wait_recv")

        @pl.when(p == 6)
        def _():
            sides(turn, cold, warm, (1, 2), "wait_recv")

    flux_ref[...] = jnp.zeros_like(flux_ref)

    def second(whole, p, carry):
        x = outer_third(p)
        takes_before(p, 0, cold_a, warm_a)
        flux = flux_ref[...]
        for r in row_groups(p):
            code = [bits[x, z, pl.ds(r, ROWS), :] for z in range(2)]
            rest = [cold_a[1, 1, 1, x + 1, z, pl.ds(r + ROWS, ROWS), :] for z in range(2)]
            sums, diffs = [], []
            for a, b, e in PAIRS:
                ahead = arrive(cold_a, x, r, code, (a, b, e))
                back = arrive(cold_a, x, r, code, (-a, -b, -e))
                sums.append([ahead[z] + back[z] for z in range(2)])
                diffs.append([ahead[z] - back[z] for z in range(2)])
            heat = [arrive_heat(warm_a, x, r, j) for j in range(7)]
            for z in range(2):
                fluid = kind[x + 1, z, pl.ds(r + ROWS, ROWS), :] == 0
                out_rest, pairs, hot = collide(
                    rest[z], [s[z] for s in sums], [d[z] for d in diffs], [g[z] for g in heat], fluid
                )
                if not whole:
                    out_rest, pairs = rest[z], [(s[z], d[z]) for s, d in zip(sums, diffs)]
                store_flow(cold_b, x, r, z, out_rest, pairs)
                store_heat(warm_b, x, r, z, hot)
                terms = []
                for j in range(1, 7):
                    was = warm_a[j, x + 1, z, pl.ds(r + ROWS, ROWS), :]
                    terms.append(weights[j - 1, x, z, pl.ds(r, ROWS), :] * (was + hot[j]))
                flux = flux + tree(terms)
        flux_ref[...] = flux
        wall_rows(warm_b, x)

        if whole:
            @pl.when(p == 5)
            def _():
                faces(1, cold_b, warm_b, "start")

        return carry

    def finish(p, carry):
        x = outer_third(p)
        for r in row_groups(p):
            for z in range(2):
                here = own(x, r, z)
                sums = [cold_b[(1 + a, 1 + b, 1 + e) + here] for a, b, e in PAIRS]
                diffs = [cold_b[(1 - a, 1 - b, 1 - e) + here] for a, b, e in PAIRS]
                heat = [warm_b[(j,) + here] for j in range(7)]
                fluid = kind[x + 1, z, pl.ds(r + ROWS, ROWS), :] == 0
                rest, pairs, _ = collide(cold_b[(1, 1, 1) + here], sums, diffs, heat, fluid)
                store_flow(cold_b, x, r, z, rest, pairs)
        return carry

    late = planes // 2
    lax.fori_loop(0, late, functools.partial(second, True), 0)
    sides(1, cold_b, warm_b, (0, 3), "start")
    lax.fori_loop(late, planes, functools.partial(second, False), 0)

    def sum_copy(slots, stage, at, target):
        return pltpu.make_async_remote_copy(
            src_ref=slots.at[at], dst_ref=slots.at[at],
            send_sem=sum_send.at[stage], recv_sem=sum_recv.at[stage],
            device_id=target, device_id_type=MESH,
        )

    def column_all():
        return sum_copy(meet_column, 0, pl.ds(0, columns - 1), column_device(1))

    def layer_all():
        return sum_copy(meet_layer, 1, pl.ds(0, layers - 1), layer_device(1))

    meet_column[pl.ds(column_index, 1), :] = jnp.sum(flux_ref[...], axis=0, keepdims=True)
    for d in range(1, columns):
        sum_copy(meet_column, 0, pl.ds(column_index, 1), column_device(d)).start()
    lax.fori_loop(late, planes, finish, 0)
    sides(1, cold_b, warm_b, (1, 2), "start")

    def third(p, carry):
        x = outer_third(p)

        @pl.when(p == 0)
        def _():
            column_all().wait_recv()
            meet_layer[pl.ds(layer_index, 1), :] = jnp.sum(meet_column[...], axis=0, keepdims=True)
            for d in range(1, layers):
                sum_copy(meet_layer, 1, pl.ds(layer_index, 1), layer_device(d)).start()

        takes_before(p, 1, cold_b, warm_b)
        for r in row_groups(p):
            code = [bits[x, z, pl.ds(r, ROWS), :] for z in range(2)]
            for a in (-1, 0, 1):
                for b in (-1, 0, 1):
                    for e in (-1, 0, 1):
                        i = 9 * (a + 1) + 3 * (b + 1) + (e + 1)
                        if i == 13:
                            value = [cold_b[1, 1, 1, x + 1, z, pl.ds(r + ROWS, ROWS), :] for z in range(2)]
                        else:
                            value = arrive(cold_b, x, r, code, (a, b, e))
                        for z in range(2):
                            flow_buf[i, x, pl.ds(r, ROWS), pl.ds(z * LANES, LANES)] = value[z]
            for j in range(7):
                value = arrive_heat(warm_b, x, r, j)
                for z in range(2):
                    heat_buf[j, x, pl.ds(r, ROWS), pl.ds(z * LANES, LANES)] = value[z]

        return carry

    lax.fori_loop(0, planes, third, 0)

    layer_all().wait_recv()
    flux_out[...] = tree([meet_layer[pl.ds(n * ROWS, ROWS), :] for n in range(layers // ROWS)])

    column_all().wait_send()
    layer_all().wait_send()
    for n, dx, dy in kind_list:
        inside(dy, kind_copy(n, dx, dy).wait_send)
    for turn, cold, warm in ((0, cold_a, warm_a), (1, cold_b, warm_b)):
        faces(turn, cold, warm, "wait_send")
        sides(turn, cold, warm, (None,), "wait_send")


def out_kernel(cells, flow_ref, heat_ref, flux_ref, flow_out, heat_out, total_out, sem):
    copies = [
        pltpu.make_async_copy(flow_ref, flow_out, sem.at[0]),
        pltpu.make_async_copy(heat_ref, heat_out, sem.at[1]),
    ]
    for copy in copies:
        copy.start()
    total_out[0, 0] = jnp.sum(flux_ref[...]) * (1.0 / cells)
    for copy in copies:
        copy.wait()


def per_device(nx, ny, flow, heat, kind):
    _, planes, height, length = flow.shape
    assert length == 2 * LANES and height % ROWS == 0 and planes == 16
    assert nx % NEAR == 0 and ny % (2 * NEAR) == 0
    padded = (planes + 2, 2, height + 2 * ROWS, LANES)
    cold, warm = (3, 3, 3) + padded, (7,) + padded
    f32, i32 = jnp.float32, jnp.int32
    flow_new, heat_new, flux = pl.pallas_call(
        functools.partial(step_kernel, nx, ny),
        out_shape=(
            pltpu.VMEM(flow.shape, f32),
            pltpu.VMEM(heat.shape, f32),
            pltpu.VMEM((ROWS, LANES), f32),
        ),
        in_specs=[pl.BlockSpec(memory_space=pl.ANY)] * 3,
        out_specs=[pl.BlockSpec(memory_space=pltpu.VMEM)] * 3,
        scratch_shapes=[
            pltpu.VMEM(padded, i32),
            pltpu.VMEM((planes, 2, height, LANES), i32),
            pltpu.VMEM((6, planes, 2, height, LANES), f32),
            pltpu.VMEM(cold, f32),
            pltpu.VMEM(cold, f32),
            pltpu.VMEM(warm, f32),
            pltpu.VMEM(warm, f32),
            pltpu.VMEM((nx * ny // (NEAR * NEAR), LANES), f32),
            pltpu.VMEM((NEAR * NEAR, LANES), f32),
            pltpu.VMEM((ROWS, LANES), f32),
            pltpu.SemaphoreType.DMA((2, planes // 2)),
            pltpu.SemaphoreType.DMA((2,)),
            pltpu.SemaphoreType.DMA((2, 12)),
            pltpu.SemaphoreType.DMA((2, 24)),
            pltpu.SemaphoreType.DMA((8,)),
            pltpu.SemaphoreType.DMA((8,)),
            pltpu.SemaphoreType.DMA((2,)),
            pltpu.SemaphoreType.DMA((2,)),
        ],
        compiler_params=pltpu.CompilerParams(
            collective_id=0, has_side_effects=True, vmem_limit_bytes=44 * 1024 * 1024
        ),
    )(*[pltpu.with_memory_space_constraint(v, pltpu.HBM) for v in (flow, heat, kind)])
    cells = float(planes * nx * height * ny)
    flow_new, heat_new, total = pl.pallas_call(
        functools.partial(out_kernel, cells),
        out_shape=(
            jax.ShapeDtypeStruct(flow.shape, f32),
            jax.ShapeDtypeStruct(heat.shape, f32),
            jax.ShapeDtypeStruct((1, 1), f32),
        ),
        in_specs=[pl.BlockSpec(memory_space=pltpu.VMEM)] * 3,
        out_specs=[
            pl.BlockSpec(memory_space=pl.ANY),
            pl.BlockSpec(memory_space=pl.ANY),
            pl.BlockSpec(memory_space=pltpu.SMEM),
        ],
        scratch_shapes=[pltpu.SemaphoreType.DMA((2,))],
        compiler_params=pltpu.CompilerParams(vmem_limit_bytes=1024 * 1024),
    )(*[pltpu.with_memory_space_constraint(v, pltpu.VMEM) for v in (flow_new, heat_new, flux)])
    return flow_new, heat_new, total[0, 0]


def solution(mesh):
    return jax.shard_map(
        functools.partial(per_device, mesh.shape["gx"], mesh.shape["gy"]),
        mesh=mesh,
        in_specs=(P(None, "gx", "gy", None), P(None, "gx", "gy", None), P("gx", "gy", None)),
        out_specs=(P(None, "gx", "gy", None), P(None, "gx", "gy", None), P()),
        check_vma=False,
    )
```

```python
import functools

import jax
import jax.numpy as jnp
from jax import lax
from jax.experimental import pallas as pl
from jax.experimental.pallas import tpu as pltpu
from jax.sharding import PartitionSpec as P

MESH = pl.DeviceIdType.MESH
NEAR = 4
STEPS = 2
LANES = 128
ROWS = 8

PAIRS = [
    (a, b, e)
    for a in (-1, 0, 1)
    for b in (-1, 0, 1)
    for e in (-1, 0, 1)
    if (a, b, e) > (0, 0, 0)
]
HEAT_MOVES = [(0, 0, 0), (1, 0, 0), (-1, 0, 0), (0, 1, 0), (0, -1, 0), (0, 0, 1), (0, 0, -1)]
TAU_COOLANT = 0.5 + 4.0 * 0.05
TAU_METAL = 0.5 + 4.0 * 0.25
FACES = [(1, 0), (-1, 0)]
SIDES = [(0, 1), (0, -1)]
CORNERS = [(1, 1), (1, -1), (-1, 1), (-1, -1)]


def tree(terms):
    terms = list(terms)
    while len(terms) > 1:
        terms = [
            terms[k] + terms[k + 1] if k + 1 < len(terms) else terms[k]
            for k in range(0, len(terms), 2)
        ]
    return terms[0]


def signed(terms):
    plus = tree([value for sign, value in terms if sign > 0])
    minus = [value for sign, value in terms if sign < 0]
    return plus - tree(minus) if minus else plus


def inverse(value):
    guess = pl.reciprocal(value, approx=True)
    return guess * (2.0 - value * guess)


def lane_shift(pair, e, lane):
    if e == 0:
        return pair
    turned = [pltpu.roll(half, 1 if e == 1 else LANES - 1, 1) for half in pair]
    at_end = lane == (0 if e == 1 else LANES - 1)
    return [jnp.where(at_end, turned[1 - k], turned[k]) for k in range(2)]


def collide(rest, sums, diffs, heat, fluid):
    density = tree([rest] + sums)
    moments = [
        signed([(c[axis], diffs[k]) for k, c in enumerate(PAIRS) if c[axis] != 0])
        for axis in range(3)
    ]
    warmth = tree(heat)
    rate = inverse(0.5 + 0.15 * jnp.exp(0.5 - 0.5 * warmth))
    rate = jnp.where(fluid, rate, 0.0)
    scale = jnp.where(fluid, inverse(density) * 3.0, 0.0)
    vx, vy, vz = [moment * scale for moment in moments]
    keep = 0.5 - 0.5 * rate
    turn = jnp.where(fluid, keep, -0.5)
    weight = rate * density
    sx, sy, sz = (0.5 * vx) * vx, (0.5 * vy) * vy, (0.5 * vz) * vz
    total = sx + sy + sz
    base = 1.0 - total * (1.0 / 3.0)
    k1 = weight * (2.0 / 27.0)
    k2 = weight * (1.0 / 54.0)
    k3 = weight * (1.0 / 216.0)
    halves = {}
    speed = (vx, vy, vz)
    square = (sx, sy, sz)
    for axis in range(3):
        c = tuple(1 if n == axis else 0 for n in range(3))
        halves[c] = (k1 * (base + square[axis]), k1 * speed[axis])
    k2v = [k2 * v for v in speed]
    for m, n in ((0, 1), (0, 2), (1, 2)):
        even = k2 * (base + square[m] + square[n])
        cross = k2v[m] * speed[n]
        for sign in (1, -1):
            c = [0, 0, 0]
            c[m], c[n] = 1, sign
            halves[tuple(c)] = (
                (even + cross, k2v[m] + k2v[n]) if sign == 1 else (even - cross, k2v[m] - k2v[n])
            )
    k3v = [k3 * v for v in speed]
    even = k3 * (base + total)
    xy, xz, yz = k3v[0] * vy, k3v[0] * vz, k3v[1] * vz
    for b in (1, -1):
        outer = even + xy if b == 1 else even - xy
        inner = xz + yz if b == 1 else xz - yz
        slope = k3v[0] + k3v[1] if b == 1 else k3v[0] - k3v[1]
        for e in (1, -1):
            halves[(1, b, e)] = (
                (outer + inner, slope + k3v[2]) if e == 1 else (outer - inner, slope - k3v[2])
            )
    out_rest = (keep + keep) * rest + (weight * (8.0 / 27.0)) * base
    out_pairs = []
    for k, c in enumerate(PAIRS):
        even, odd = halves[c]
        even = keep * sums[k] + even
        odd = turn * diffs[k] + odd
        out_pairs.append((even + odd, even - odd))
    heat_rate = jnp.where(fluid, 1.0 / TAU_COOLANT, 1.0 / TAU_METAL)
    heat_keep = 1.0 - heat_rate
    part = (heat_rate * 0.125) * warmth
    slant = part * (4.0 / 3.0)
    hot = [heat_keep * heat[0] + (part + part)]
    for axis in range(3):
        lean = slant * speed[axis]
        hot.append(heat_keep * heat[1 + 2 * axis] + (part + lean))
        hot.append(heat_keep * heat[2 + 2 * axis] + (part - lean))
    return out_rest, out_pairs, hot


def step_kernel(
    nx, ny, flow_hbm, heat_hbm, kind_hbm, flow_buf, heat_buf, flux_out,
    kind, bits, weights, cold_a, cold_b, warm_a, warm_b, meet_column, meet_layer, flux_ref,
    in_sem, kind_sem, send_sem, recv_sem, kind_send, kind_recv, sum_send, sum_recv,
):
    gx, gy = lax.axis_index("gx"), lax.axis_index("gy")
    planes, height = flow_buf.shape[1], flow_buf.shape[2]
    lane = lax.broadcasted_iota(jnp.int32, (ROWS, LANES), 1)
    half = height // ROWS
    low_row, high_row = ROWS, ROWS + height - 1

    def outer_first(p):
        k = p // 2
        return lax.rem(p, 2) * (planes - 1 - k) + (1 - lax.rem(p, 2)) * k

    def outer_third(p):
        k = p // 2
        k = jnp.where(k < 3, lax.rem(k + 1, 3), k)
        return lax.rem(p, 2) * (planes - 1 - k) + (1 - lax.rem(p, 2)) * k

    def row_groups(p):
        low = lax.shift_right_logical(p, 6) * ROWS
        return [pl.multiple_of(low + h * ROWS, ROWS) for h in range(half)]

    def device(dx, dy):
        return (lax.rem(gx + dx + nx, nx), lax.rem(gy + dy + ny, ny))

    def inside(dy, act):
        if dy == 1:
            pl.when(gy < ny - 1)(act)
        elif dy == -1:
            pl.when(gy > 0)(act)
        else:
            act()

    along, across = gx // NEAR, lax.rem(gx, NEAR)
    far, near, core = gy // (2 * NEAR), lax.rem(gy, 2 * NEAR) // 2, lax.rem(gy, 2)
    fars = ny // (2 * NEAR)
    columns = 2 * fars * (nx // NEAR)
    layers = NEAR * NEAR
    column_index = (along * fars + far) * 2 + core
    layer_index = across * NEAR + near

    def column_device(d):
        n = lax.rem(column_index + d, columns)
        return ((n // (2 * fars)) * NEAR + across, (lax.rem(n, 2 * fars) // 2) * 2 * NEAR + near * 2 + lax.rem(n, 2))

    def layer_device(d):
        n = lax.rem(layer_index + d, layers)
        return (along * NEAR + n // NEAR, far * 2 * NEAR + lax.rem(n, NEAR) * 2 + core)

    barrier = pltpu.get_barrier_semaphore()
    greeted = [device(dx, dy) for dx, dy in FACES + SIDES + CORNERS]
    greeted += [column_device(d) for d in range(1, columns)]
    greeted += [layer_device(d) for d in range(1, layers)]
    for target in greeted:
        pl.semaphore_signal(barrier, inc=1, device_id=target, device_id_type=MESH)

    kind_copies = [
        pltpu.make_async_copy(
            kind_hbm.at[:, :, pl.ds(z * LANES, LANES)],
            kind.at[pl.ds(1, planes), z, pl.ds(low_row, height), :],
            kind_sem.at[z],
        )
        for z in range(2)
    ]
    for copy in kind_copies:
        copy.start()

    def load(k):
        xs = pl.ds(2 * k, 2)
        return [
            pltpu.make_async_copy(flow_hbm.at[:, xs], flow_buf.at[:, xs], in_sem.at[0, k]),
            pltpu.make_async_copy(heat_hbm.at[:, xs], heat_buf.at[:, xs], in_sem.at[1, k]),
        ]

    for k in range(planes // 4):
        for copy in load(k) + load(planes // 2 - 1 - k):
            copy.start()

    for copy in kind_copies:
        copy.wait()

    def spans(dx, dy, xs):
        src_x = {1: pl.ds(planes, 1), -1: pl.ds(1, 1), 0: xs}[dx]
        dst_x = {1: pl.ds(0, 1), -1: pl.ds(planes + 1, 1), 0: xs}[dx]
        src_y = {1: pl.ds(high_row, 1), -1: pl.ds(low_row, 1), 0: pl.ds(low_row, height)}[dy]
        dst_y = {1: pl.ds(low_row - 1, 1), -1: pl.ds(high_row + 1, 1), 0: pl.ds(low_row, height)}[dy]
        return (src_x, src_y), (dst_x, dst_y)

    def remote(src, dst, send, recv, dx, dy):
        return pltpu.make_async_remote_copy(
            src_ref=src, dst_ref=dst, send_sem=send, recv_sem=recv,
            device_id=device(dx, dy), device_id_type=MESH,
        )

    every = pl.ds(1, planes)

    def kind_copy(n, dx, dy):
        (sx, sy), (tx, ty) = spans(dx, dy, every)
        return remote(
            kind.at[sx, :, sy, :], kind.at[tx, :, ty, :], kind_send.at[n], kind_recv.at[n], dx, dy
        )

    kind_list = [(n, dx, dy) for n, (dx, dy) in enumerate(FACES + SIDES + CORNERS)]

    def moving(cold, dx, dy, xs, ys):
        a = dx + 1 if dx else slice(None)
        b = dy + 1 if dy else slice(None)
        return cold.at[a, b, :, xs, :, ys, :]

    def flow_copy(turn, cold, dx, dy, send, recv, xs=every):
        (sx, sy), (tx, ty) = spans(dx, dy, xs)
        return remote(
            moving(cold, dx, dy, sx, sy), moving(cold, dx, dy, tx, ty),
            send_sem.at[turn, send], recv_sem.at[turn, recv], dx, dy,
        )

    def heat_copy(turn, warm, dx, dy, send, recv, xs=every):
        j = HEAT_MOVES.index((dx, dy, 0))
        (sx, sy), (tx, ty) = spans(dx, dy, xs)
        return remote(
            warm.at[j, sx, :, sy, :], warm.at[j, tx, :, ty, :],
            send_sem.at[turn, send], recv_sem.at[turn, recv], dx, dy,
        )

    def face_copies(turn, cold, warm, n):
        dx, _ = FACES[n]
        return [
            flow_copy(turn, cold, dx, 0, 2 * n, 2 * n),
            heat_copy(turn, warm, dx, 0, 2 * n + 1, 2 * n + 1),
        ]

    def corner_copy(turn, cold, n):
        dx, dy = CORNERS[n]
        return flow_copy(turn, cold, dx, dy, 4 + n, 4 + n)

    group = planes // 4

    def side_copies(turn, cold, warm, n, g=None):
        _, dy = SIDES[n]
        xs = every if g is None else pl.ds(1 + group * g, group)
        recv = 8 + 2 * (4 * n + (0 if g is None else g))
        return [
            flow_copy(turn, cold, 0, dy, 8 + 2 * n, recv, xs),
            heat_copy(turn, warm, 0, dy, 9 + 2 * n, recv + 1, xs),
        ]

    def each(copies, what):
        def act():
            for copy in copies:
                getattr(copy, what)()
        return act

    def faces(turn, cold, warm, what):
        sign = -1 if what == "wait_recv" else 1
        for n in range(2):
            each(face_copies(turn, cold, warm, n), what)()
        for n in range(4):
            inside(sign * CORNERS[n][1], each([corner_copy(turn, cold, n)], what))

    def sides(turn, cold, warm, gs, what):
        sign = -1 if what == "wait_recv" else 1
        for n in range(2):
            copies = [c for g in gs for c in side_copies(turn, cold, warm, n, g)]
            inside(sign * SIDES[n][1], each(copies, what))

    def own(x, r, z):
        return (x + 1, z, pl.ds(r + ROWS, ROWS), slice(None))

    def store_flow(cold, x, r, z, rest, pairs):
        here = own(x, r, z)
        cold[(1, 1, 1) + here] = rest
        for (a, b, e), (ahead, back) in zip(PAIRS, pairs):
            cold[(1 + a, 1 + b, 1 + e) + here] = ahead
            cold[(1 - a, 1 - b, 1 - e) + here] = back

    def store_heat(warm, x, r, z, hot):
        for j in range(7):
            warm[(j,) + own(x, r, z)] = hot[j]

    def wall_rows(warm, x):
        @pl.when(gy == 0)
        def _():
            for z in range(2):
                warm[3, x + 1, z, pl.ds(low_row - 1, 1), :] = warm[4, x + 1, z, pl.ds(low_row, 1), :]

        @pl.when(gy == ny - 1)
        def _():
            for z in range(2):
                warm[4, x + 1, z, pl.ds(high_row + 1, 1), :] = warm[3, x + 1, z, pl.ds(high_row, 1), :]

    def outside_rows(row):
        def act():
            kind[:, :, pl.ds(row, 1), :] = jnp.full((planes + 2, 2, 1, LANES), 2, jnp.int32)
        return act

    together = 2

    def mask(q, carry):
        for x in [q * together + n for n in range(together)]:
            for r in row_groups(q):
                own = [kind[x + 1, z, pl.ds(r + ROWS, ROWS), :] for z in range(2)]
                lines, near = [], []
                for z in range(2):
                    found = {}
                    for a in (-1, 0, 1):
                        for b in (-1, 0, 1):
                            value = own[z] if a == b == 0 else kind[x + 1 - a, z, pl.ds(r + ROWS - b, ROWS), :]
                            found[a, b] = value
                    near.append([found[-1, 0], found[1, 0], found[0, -1], found[0, 1]])
                    lines.append(tree([
                        jnp.where(found[a, b] == 0, 1 << (9 * (a + 1) + 3 * (b + 1)), 0)
                        for a in (-1, 0, 1) for b in (-1, 0, 1)
                    ]))
                above = lane_shift(lines, -1, lane)
                below = lane_shift(lines, 1, lane)
                for z in range(2):
                    code = above[z] + (lines[z] << 1) + (below[z] << 2)
                    bits[x, z, pl.ds(r, ROWS), :] = jnp.where(own[z] == 0, code, 0)
                    others = [jnp.where(v == 2, own[z], v) for v in near[z]]
                    others += [1 - ((v[z] >> 12) & 1) for v in (above, below)]
                    for j in range(6):
                        weights[j, x, z, pl.ds(r, ROWS), :] = (own[z] - others[j]).astype(jnp.float32)
        return carry

    def first(p, carry):
        x = outer_first(p)

        @pl.when(lax.rem(p, 4) < 2)
        def _():
            for copy in load(x // 2):
                copy.wait()

        @pl.when(p == 3)
        def _():
            pl.semaphore_wait(barrier, len(greeted))
            for n, dx, dy in kind_list:
                inside(dy, kind_copy(n, dx, dy).start)

        for r in row_groups(p):
            for z in range(2):
                at = (x, pl.ds(r, ROWS), pl.ds(z * LANES, LANES))
                values = [flow_buf[(i,) + at] for i in range(27)]
                heat = [heat_buf[(j,) + at] for j in range(7)]
                fluid = kind[x + 1, z, pl.ds(r + ROWS, ROWS), :] == 0
                sums = [values[i] + values[26 - i] for i in range(14, 27)]
                diffs = [values[i] - values[26 - i] for i in range(14, 27)]
                rest, pairs, hot = collide(values[13], sums, diffs, heat, fluid)
                store_flow(cold_a, x, r, z, rest, pairs)
                store_heat(warm_a, x, r, z, hot)
        wall_rows(warm_a, x)

        @pl.when(p == 3)
        def _():
            faces(0, cold_a, warm_a, "start")

        @pl.when(p == planes // 2 - 1)
        def _():
            sides(0, cold_a, warm_a, (0, 3), "start")

        return carry

    lax.fori_loop(0, planes, first, 0)
    sides(0, cold_a, warm_a, (1, 2), "start")

    for n, dx, dy in kind_list:
        inside(-dy, kind_copy(n, dx, dy).wait_recv)
    pl.when(gy == 0)(outside_rows(low_row - 1))
    pl.when(gy == ny - 1)(outside_rows(high_row + 1))
    lax.fori_loop(0, planes // together, mask, 0)

    def arrive(cold, x, r, code, c):
        a, b, e = c
        number = 9 * (a + 1) + 3 * (b + 1) + (e + 1)
        found = lane_shift(
            [cold[a + 1, b + 1, e + 1, x + 1 - a, z, pl.ds(r + ROWS - b, ROWS), :] for z in range(2)],
            e, lane,
        )
        return [
            jnp.where(
                (code[z] & (1 << number)) != 0,
                found[z],
                cold[1 - a, 1 - b, 1 - e, x + 1, z, pl.ds(r + ROWS, ROWS), :],
            )
            for z in range(2)
        ]

    def arrive_heat(warm, x, r, j):
        a, b, e = HEAT_MOVES[j]
        found = [warm[j, x + 1 - a, z, pl.ds(r + ROWS - b, ROWS), :] for z in range(2)]
        return lane_shift(found, e, lane)

    def takes_before(p, turn, cold, warm):
        @pl.when(p == 0)
        def _():
            sides(turn, cold, warm, (0, 3), "wait_recv")

        @pl.when(p == 4)
        def _():
            faces(turn, cold, warm, "wait_recv")

        @pl.when(p == 6)
        def _():
            sides(turn, cold, warm, (1, 2), "wait_recv")

    flux_ref[...] = jnp.zeros_like(flux_ref)

    def second(whole, p, carry):
        x = outer_third(p)
        takes_before(p, 0, cold_a, warm_a)
        flux = flux_ref[...]
        for r in row_groups(p):
            code = [bits[x, z, pl.ds(r, ROWS), :] for z in range(2)]
            rest = [cold_a[1, 1, 1, x + 1, z, pl.ds(r + ROWS, ROWS), :] for z in range(2)]
            sums, diffs = [], []
            for a, b, e in PAIRS:
                ahead = arrive(cold_a, x, r, code, (a, b, e))
                back = arrive(cold_a, x, r, code, (-a, -b, -e))
                sums.append([ahead[z] + back[z] for z in range(2)])
                diffs.append([ahead[z] - back[z] for z in range(2)])
            heat = [arrive_heat(warm_a, x, r, j) for j in range(7)]
            for z in range(2):
                fluid = kind[x + 1, z, pl.ds(r + ROWS, ROWS), :] == 0
                out_rest, pairs, hot = collide(
                    rest[z], [s[z] for s in sums], [d[z] for d in diffs], [g[z] for g in heat], fluid
                )
                if not whole:
                    out_rest, pairs = rest[z], [(s[z], d[z]) for s, d in zip(sums, diffs)]
                store_flow(cold_b, x, r, z, out_rest, pairs)
                store_heat(warm_b, x, r, z, hot)
                terms = []
                for j in range(1, 7):
                    was = warm_a[j, x + 1, z, pl.ds(r + ROWS, ROWS), :]
                    terms.append(weights[j - 1, x, z, pl.ds(r, ROWS), :] * (was + hot[j]))
                flux = flux + tree(terms)
        flux_ref[...] = flux
        wall_rows(warm_b, x)

        if whole:
            @pl.when(p == 5)
            def _():
                faces(1, cold_b, warm_b, "start")

        return carry

    def finish(p, carry):
        x = outer_third(p)
        for r in row_groups(p):
            for z in range(2):
                here = own(x, r, z)
                sums = [cold_b[(1 + a, 1 + b, 1 + e) + here] for a, b, e in PAIRS]
                diffs = [cold_b[(1 - a, 1 - b, 1 - e) + here] for a, b, e in PAIRS]
                heat = [warm_b[(j,) + here] for j in range(7)]
                fluid = kind[x + 1, z, pl.ds(r + ROWS, ROWS), :] == 0
                rest, pairs, _ = collide(cold_b[(1, 1, 1) + here], sums, diffs, heat, fluid)
                store_flow(cold_b, x, r, z, rest, pairs)
        return carry

    late = planes // 2
    lax.fori_loop(0, late, functools.partial(second, True), 0)
    sides(1, cold_b, warm_b, (0, 3), "start")
    lax.fori_loop(late, planes, functools.partial(second, False), 0)

    def sum_copy(slots, stage, at, target):
        return pltpu.make_async_remote_copy(
            src_ref=slots.at[at], dst_ref=slots.at[at],
            send_sem=sum_send.at[stage], recv_sem=sum_recv.at[stage],
            device_id=target, device_id_type=MESH,
        )

    def column_all():
        return sum_copy(meet_column, 0, pl.ds(0, columns - 1), column_device(1))

    def layer_all():
        return sum_copy(meet_layer, 1, pl.ds(0, layers - 1), layer_device(1))

    meet_column[pl.ds(column_index, 1), :] = jnp.sum(flux_ref[...], axis=0, keepdims=True)
    for d in range(1, columns):
        sum_copy(meet_column, 0, pl.ds(column_index, 1), column_device(d)).start()
    lax.fori_loop(late, planes, finish, 0)
    sides(1, cold_b, warm_b, (1, 2), "start")

    def third(p, carry):
        x = outer_third(p)

        @pl.when(p == 0)
        def _():
            column_all().wait_recv()
            meet_layer[pl.ds(layer_index, 1), :] = jnp.sum(meet_column[...], axis=0, keepdims=True)
            for d in range(1, layers):
                sum_copy(meet_layer, 1, pl.ds(layer_index, 1), layer_device(d)).start()

        takes_before(p, 1, cold_b, warm_b)
        for r in row_groups(p):
            code = [bits[x, z, pl.ds(r, ROWS), :] for z in range(2)]
            for a in (-1, 0, 1):
                for b in (-1, 0, 1):
                    for e in (-1, 0, 1):
                        i = 9 * (a + 1) + 3 * (b + 1) + (e + 1)
                        if i == 13:
                            value = [cold_b[1, 1, 1, x + 1, z, pl.ds(r + ROWS, ROWS), :] for z in range(2)]
                        else:
                            value = arrive(cold_b, x, r, code, (a, b, e))
                        for z in range(2):
                            flow_buf[i, x, pl.ds(r, ROWS), pl.ds(z * LANES, LANES)] = value[z]
            for j in range(7):
                value = arrive_heat(warm_b, x, r, j)
                for z in range(2):
                    heat_buf[j, x, pl.ds(r, ROWS), pl.ds(z * LANES, LANES)] = value[z]

        return carry

    lax.fori_loop(0, planes, third, 0)

    column_all().wait_send()
    for n, dx, dy in kind_list:
        inside(dy, kind_copy(n, dx, dy).wait_send)
    for turn, cold, warm in ((0, cold_a, warm_a), (1, cold_b, warm_b)):
        faces(turn, cold, warm, "wait_send")
        sides(turn, cold, warm, (None,), "wait_send")

    layer_all().wait_recv()
    flux_out[...] = tree([meet_layer[pl.ds(n * ROWS, ROWS), :] for n in range(layers // ROWS)])

    layer_all().wait_send()


def out_kernel(cells, flow_ref, heat_ref, flux_ref, flow_out, heat_out, total_out, sem):
    copies = [
        pltpu.make_async_copy(flow_ref, flow_out, sem.at[0]),
        pltpu.make_async_copy(heat_ref, heat_out, sem.at[1]),
    ]
    for copy in copies:
        copy.start()
    total_out[0, 0] = jnp.sum(flux_ref[...]) * (1.0 / cells)
    for copy in copies:
        copy.wait()


def per_device(nx, ny, flow, heat, kind):
    _, planes, height, length = flow.shape
    assert length == 2 * LANES and height % ROWS == 0 and planes == 16
    assert nx % NEAR == 0 and ny % (2 * NEAR) == 0
    padded = (planes + 2, 2, height + 2 * ROWS, LANES)
    cold, warm = (3, 3, 3) + padded, (7,) + padded
    f32, i32 = jnp.float32, jnp.int32
    flow_new, heat_new, flux = pl.pallas_call(
        functools.partial(step_kernel, nx, ny),
        out_shape=(
            pltpu.VMEM(flow.shape, f32),
            pltpu.VMEM(heat.shape, f32),
            pltpu.VMEM((ROWS, LANES), f32),
        ),
        in_specs=[pl.BlockSpec(memory_space=pl.ANY)] * 3,
        out_specs=[pl.BlockSpec(memory_space=pltpu.VMEM)] * 3,
        scratch_shapes=[
            pltpu.VMEM(padded, i32),
            pltpu.VMEM((planes, 2, height, LANES), i32),
            pltpu.VMEM((6, planes, 2, height, LANES), f32),
            pltpu.VMEM(cold, f32),
            pltpu.VMEM(cold, f32),
            pltpu.VMEM(warm, f32),
            pltpu.VMEM(warm, f32),
            pltpu.VMEM((nx * ny // (NEAR * NEAR), LANES), f32),
            pltpu.VMEM((NEAR * NEAR, LANES), f32),
            pltpu.VMEM((ROWS, LANES), f32),
            pltpu.SemaphoreType.DMA((2, planes // 2)),
            pltpu.SemaphoreType.DMA((2,)),
            pltpu.SemaphoreType.DMA((2, 12)),
            pltpu.SemaphoreType.DMA((2, 24)),
            pltpu.SemaphoreType.DMA((8,)),
            pltpu.SemaphoreType.DMA((8,)),
            pltpu.SemaphoreType.DMA((2,)),
            pltpu.SemaphoreType.DMA((2,)),
        ],
        compiler_params=pltpu.CompilerParams(
            collective_id=0, has_side_effects=True, vmem_limit_bytes=44 * 1024 * 1024
        ),
    )(*[pltpu.with_memory_space_constraint(v, pltpu.HBM) for v in (flow, heat, kind)])
    cells = float(planes * nx * height * ny)
    flow_new, heat_new, total = pl.pallas_call(
        functools.partial(out_kernel, cells),
        out_shape=(
            jax.ShapeDtypeStruct(flow.shape, f32),
            jax.ShapeDtypeStruct(heat.shape, f32),
            jax.ShapeDtypeStruct((1, 1), f32),
        ),
        in_specs=[pl.BlockSpec(memory_space=pltpu.VMEM)] * 3,
        out_specs=[
            pl.BlockSpec(memory_space=pl.ANY),
            pl.BlockSpec(memory_space=pl.ANY),
            pl.BlockSpec(memory_space=pltpu.SMEM),
        ],
        scratch_shapes=[pltpu.SemaphoreType.DMA((2,))],
        compiler_params=pltpu.CompilerParams(vmem_limit_bytes=1024 * 1024),
    )(*[pltpu.with_memory_space_constraint(v, pltpu.VMEM) for v in (flow_new, heat_new, flux)])
    return flow_new, heat_new, total[0, 0]


def solution(mesh):
    return jax.shard_map(
        functools.partial(per_device, mesh.shape["gx"], mesh.shape["gy"]),
        mesh=mesh,
        in_specs=(P(None, "gx", "gy", None), P(None, "gx", "gy", None), P("gx", "gy", None)),
        out_specs=(P(None, "gx", "gy", None), P(None, "gx", "gy", None), P()),
        check_vma=False,
    )
```
